512 devices in a mesh: slab: 16 (over z, core), fib: 32 (over x, y).
Axes of the slice: x: 4, y: 8, z: 8, core: 2. Of those that a mesh axis runs over, the one named last changes fastest.
Arguments:
- values: bfloat16 [16, 64, 64, 4096], P('slab', 'fib'), may hold values from -6 to 6
- observed: int32 [16, 64, 64, 4096], P('slab', 'fib'), may hold values 0 or 1
- coords: int32 [16, 64, 3], P('slab', 'fib'), may hold values from 0 to 31, as said below
- counts: int32 [16, 32], P('slab', 'fib'), may hold values from 1 to 2, as said below
- item_factors: float32 [4096, 32], P('fib'), may hold values from -6 to 6
- week_factors: float32 [2048, 32], P(('slab', 'fib')), may hold values from -0.06 to 0.06
Outputs:
- user_factors: float32 [4096, 32], P(('slab', 'fib'))
- item_updated: float32 [4096, 32], P('fib')
The draws below stay inside these ranges and needn't reach their ends.
Inputs may be any that keep to these rules, and one draw needn't show every extreme that they name: `coords`: each row is a user block below 4, an item block below 2 and a week block below 32; the 2 rows of one device are distinct. `counts`: each device holds 1 or 2 live slots, its first ones; some device holds 2.
All inputs are finite; a program needn't handle non-finite values. No bound on the sum of `observed` on one device may be relied on, other than what follows from the above.
Results may differ from the reference program's by a relative error of at most 0.0029.
Values may be sent and summed in bfloat16 or wider, within the bound.
No kernel may reach another device: no remote copies, remote signals or barrier semaphores. Data moves between devices by JAX's collectives and lax.ppermute only.
A program may use at most 64 MiB of HBM per device.

```python
import jax
import jax.numpy as jnp
from jax import lax

B = 64
R = 32
UBD = 4
IBD = 2
NWB = 32
NB = 2
NU = 4096
NI = 4096
NW = 2048
N_SLAB = 16
N_FIB = 32


def draw_coords(key, part):
    key = jax.random.fold_in(key, 7)
    options = UBD * IBD * NWB
    keys = jax.random.split(key, N_SLAB * N_FIB)

    def pick_some(single):
        return jax.random.permutation(single, options)[:NB].astype(jnp.int32)
    picked = jax.vmap(pick_some)(keys)
    first_key = jax.random.fold_in(key, 1)
    inner = (jax.random.permutation(first_key, options - 2)[:NB - 2] + 1).astype(jnp.int32)
    leading = jnp.concatenate([jnp.array([options - 1, 0], dtype=jnp.int32), inner])
    picked = picked.at[0].set(leading)
    user_part = picked // (IBD * NWB)
    item_part = picked // NWB % IBD
    week_part = picked % NWB
    stacked = jnp.stack([user_part, item_part, week_part], axis=-1).astype(jnp.int32)
    return stacked.reshape(N_SLAB, N_FIB * NB, 3)


def draw_counts(key, part):
    key = jax.random.fold_in(key, 11)
    picks = jax.random.randint(key, (N_SLAB, N_FIB), 0, 4)
    filled = jnp.where(picks == 0, NB, 1).astype(jnp.int32)
    return filled.at[0, 0].set(NB)


def touch_ends(values, own_key, smallest, largest):
    place = [jax.random.randint(jax.random.fold_in(own_key, axis), (), 0, length) for axis, length in enumerate(values.shape)]
    main_axis = values.shape.index(max(values.shape))
    neighbour = place[:main_axis] + [(place[main_axis] + 1) % values.shape[main_axis]] + place[main_axis + 1:]
    return values.at[tuple(place)].set(smallest).at[tuple(neighbour)].set(largest)


def shard_levels(key, shape, shards, low, top_value):
    level, own = 1.0, jax.random.fold_in(key, 6)
    for position, parts in shards:
        draws = jnp.exp(jax.random.uniform(jax.random.fold_in(own, position), (parts,), jnp.float32, low / len(shards), top_value / len(shards)))
        level = level * jnp.repeat(draws, shape[position] // parts).reshape([-1 if axis == position else 1 for axis in range(len(shape))])
    return level


def normal_values(own_key, shape, deviation, bound, cuts=(), kind=jnp.bfloat16):
    entries = jax.random.normal(own_key, shape, jnp.float32) * deviation
    if len(cuts) > 0:
        entries = shard_levels(own_key, shape, cuts, -0.22, 0.18) * entries
    return jnp.clip(entries, min=-bound, max=bound).astype(kind)


def setup_inputs(seed: int = 0) -> dict:
    splits = jax.random.split(jax.random.key(seed), 7)
    values = normal_values(splits[0], (N_SLAB, N_FIB * NB, B, B * B), 1.0, 6.0, ((0, 16), (1, 32)))
    observed = touch_ends((jax.random.randint(splits[1], (N_SLAB, N_FIB * NB, B, B * B), 0, 10) < 3).astype(jnp.int32), jax.random.fold_in(splits[1], 1), 0, 1)
    coords = draw_coords(jax.random.fold_in(splits[6], 71), 0)
    counts = draw_counts(jax.random.fold_in(splits[6], 71), 0)
    item_factors = normal_values(splits[4], (NI, R), 1.0, 6.0, ((0, 32),), jnp.float32)
    week_factors = normal_values(splits[5], (NW, R), 0.01, 0.06, ((0, 512),), jnp.float32)
    return dict(values=values, observed=observed, coords=coords, counts=counts, item_factors=item_factors, week_factors=week_factors)


ridge_weight = 1.0
precise = lax.Precision.HIGHEST

def pair_table(rows):
    return (rows[:, :, None] * rows[:, None, :]).reshape(rows.shape[0], -1)

def ridge_solve(gram, rhs):
    count, width = rhs.shape
    system = gram.reshape(count, width, width) + ridge_weight * jnp.eye(width, dtype=jnp.float32)
    factor = jnp.linalg.cholesky(system)
    return jax.scipy.linalg.cho_solve((factor, True), rhs[:, :, None])[:, :, 0]

def block_terms(block_vals, block_mask, week_rows, pair_rows):
    mask_half = block_mask.astype(jnp.bfloat16)
    weighted = block_vals * mask_half
    mask_cube = mask_half.reshape(B, B, B).astype(jnp.float32)
    value_cube = weighted.reshape(B, B, B).astype(jnp.float32)
    cross = jnp.einsum('uiw,wk->uik', mask_cube, pair_rows.astype(jnp.float32), precision=precise)
    moment = jnp.einsum('uiw,wr->uir', value_cube, week_rows.astype(jnp.float32), precision=precise)
    return (cross, moment)

def reference(values, observed, coords, counts, item_factors, week_factors):
    weeks_half = week_factors.astype(jnp.bfloat16)
    week_pairs = pair_table(weeks_half.astype(jnp.float32)).astype(jnp.bfloat16)
    slots = N_FIB * NB
    total = N_SLAB * slots
    flat_vals = values.reshape(total, B, B * B)
    flat_mask = observed.reshape(total, B, B * B)
    flat_coords = coords.reshape(total, 3)
    order = jnp.arange(total, dtype=jnp.int32)
    slab_of = order // slots
    fib_of = order % slots // NB
    weight = (order % NB < counts[slab_of, fib_of]).astype(jnp.float32)
    user_base = (slab_of * (UBD * B) + flat_coords[:, 0] * B).astype(jnp.int32)
    item_base = (fib_of * (IBD * B) + flat_coords[:, 1] * B).astype(jnp.int32)
    week_base = (flat_coords[:, 2] * B).astype(jnp.int32)
    width = R * R
    item_pairs = pair_table(item_factors)
    inputs = (flat_vals, flat_mask, user_base, item_base, week_base, weight)

    def user_step(carry, slot):
        gram, rhs = carry
        block_vals, block_mask, ubase, ibase, wbase, alive = slot
        week_rows = lax.dynamic_slice_in_dim(weeks_half, wbase, B, 0)
        pair_rows = lax.dynamic_slice_in_dim(week_pairs, wbase, B, 0)
        cross, moment = block_terms(block_vals, block_mask, week_rows, pair_rows)
        ipairs = lax.dynamic_slice_in_dim(item_pairs, ibase, B, 0)
        irows = lax.dynamic_slice_in_dim(item_factors, ibase, B, 0)
        gram_add = jnp.einsum('uik,ik->uk', cross, ipairs, precision=precise) * alive
        rhs_add = jnp.einsum('uir,ir->ur', moment, irows, precision=precise) * alive
        gram = lax.dynamic_update_slice_in_dim(gram, lax.dynamic_slice_in_dim(gram, ubase, B, 0) + gram_add, ubase, 0)
        rhs = lax.dynamic_update_slice_in_dim(rhs, lax.dynamic_slice_in_dim(rhs, ubase, B, 0) + rhs_add, ubase, 0)
        return ((gram, rhs), None)
    start = (jnp.zeros((NU, width), jnp.float32), jnp.zeros((NU, R), jnp.float32))
    (user_gram, user_rhs), _ = lax.scan(user_step, start, inputs)
    user_factors = ridge_solve(user_gram, user_rhs)
    user_pairs = pair_table(user_factors)

    def item_step(carry, slot):
        gram, rhs = carry
        block_vals, block_mask, ubase, ibase, wbase, alive = slot
        week_rows = lax.dynamic_slice_in_dim(weeks_half, wbase, B, 0)
        pair_rows = lax.dynamic_slice_in_dim(week_pairs, wbase, B, 0)
        cross, moment = block_terms(block_vals, block_mask, week_rows, pair_rows)
        upairs = lax.dynamic_slice_in_dim(user_pairs, ubase, B, 0)
        urows = lax.dynamic_slice_in_dim(user_factors, ubase, B, 0)
        gram_add = jnp.einsum('uik,uk->ik', cross, upairs, precision=precise) * alive
        rhs_add = jnp.einsum('uir,ur->ir', moment, urows, precision=precise) * alive
        gram = lax.dynamic_update_slice_in_dim(gram, lax.dynamic_slice_in_dim(gram, ibase, B, 0) + gram_add, ibase, 0)
        rhs = lax.dynamic_update_slice_in_dim(rhs, lax.dynamic_slice_in_dim(rhs, ibase, B, 0) + rhs_add, ibase, 0)
        return ((gram, rhs), None)
    start = (jnp.zeros((NI, width), jnp.float32), jnp.zeros((NI, R), jnp.float32))
    (item_gram, item_rhs), _ = lax.scan(item_step, start, inputs)
    item_updated = ridge_solve(item_gram, item_rhs)
    return (user_factors, item_updated)
```

```python
import jax
import jax.numpy as jnp
import numpy as np
from jax import lax
from jax.experimental import pallas as pl
from jax.experimental.pallas import tpu as pltpu
from jax.sharding import PartitionSpec as P

B = 64
R = 32
UBD = 4
IBD = 2
T = 8
LANES = 128
SIDE = 4
CHUNK = SIDE * B
PACK = LANES // R
WROWS = B // PACK
ridge_weight = 1.0
precise = lax.Precision.HIGHEST
LINK = jnp.bfloat16
f32 = jnp.float32
bf16 = jnp.bfloat16


def tables():
    start, left, right = {}, [], []
    for r in range(R):
        start[r] = len(left)
        for s in range(r // T * T, R):
            left.append(r)
            right.append(s)
    width = len(left)
    one = np.zeros((R, width), np.float32)
    two = np.zeros((R, width), np.float32)
    for k, (r, s) in enumerate(zip(left, right)):
        if s >= r:
            one[r, k] = 1
            two[s, k] = 1
    put = np.zeros((LANES, width), np.float32)
    for j in range(R // T):
        row5, row6, row7 = (start[j * T + n] for n in (5, 6, 7))
        for n in range(7):
            put[j * T + n, row7 + n] = 1
        put[j * T + 7, row6] = 1
        for n in range(1, 6):
            put[R + j * T + n, row6 + n] = 1
        put[R + j * T, row5] = 1
        put[R + j * T + 6, row5 + 1] = 1
        put[R + j * T + 7, row5 + 2] = 1
    return start, width, one, two, put


START, WIDTH, ONE, TWO, PUT = tables()


def dot(a, b, dims=(1, 0), precision=None):
    return lax.dot_general(
        a, b, (((dims[0],), (dims[1],)), ((), ())), preferred_element_type=f32, precision=precision
    )


def iota(shape, dim):
    return lax.broadcasted_iota(jnp.int32, shape, dim)


def week_block(weeks, wide_one, wide_two, start):
    packed = weeks[pl.ds(pl.multiple_of(start * WROWS, WROWS), WROWS), :]
    spread = (iota((B, WROWS), 0) // PACK == iota((B, WROWS), 1)).astype(f32).astype(bf16)
    rows = dot(spread, packed)
    own = iota((B, LANES), 0) % PACK == iota((B, LANES), 1) // R
    rows = jnp.where(own, rows, 0.0).astype(bf16)
    pairs = (dot(rows, wide_one[...]) * dot(rows, wide_two[...])).astype(bf16).astype(f32)
    fold = (iota((LANES, LANES), 0) % R == iota((LANES, LANES), 1) % R).astype(f32).astype(bf16)
    return pairs, dot(rows, fold)


def split(x):
    high = x.astype(bf16).astype(f32)
    return jnp.where(iota(x.shape, 1) < R, high, x - high).astype(bf16)


def repeat_rows(rows):
    return jnp.concatenate([rows] * PACK, axis=1)


def join(x):
    return x[:, :R] + x[:, R:2 * R]


def send_form(gram, rhs, put):
    parts = split(repeat_rows(rhs))
    parts = jnp.where(iota(parts.shape, 1) < 2 * R, parts.astype(f32), 0.0).astype(bf16)
    return (gram + dot(parts, put[...])).astype(LINK)


def block_arrays(values, observed, slot):
    mask = observed[slot].astype(f32)
    return mask.astype(bf16), (values[slot].astype(f32) * mask).astype(bf16)


def user_kernel(coords, counts, values, observed, items, weeks, one, two, wide_one, wide_two, put, out, gram, rhs):
    gram[...] = jnp.zeros_like(gram)
    rhs[...] = jnp.zeros_like(rhs)

    def block(slot):
        ubase = pl.multiple_of(coords[slot, 0] * B, B)
        ibase = pl.multiple_of(coords[slot, 1] * B, B)
        wpairs, wrows = week_block(weeks, wide_one, wide_two, coords[slot, 2])
        rows = items[pl.ds(ibase, B), :]
        ipairs = dot(rows, one[...], precision=precise) * dot(rows, two[...], precision=precise)
        irows = repeat_rows(rows)
        mask, weighted = block_arrays(values, observed, slot)
        gram_add = jnp.zeros((B, WIDTH), f32)
        rhs_add = jnp.zeros((B, LANES), f32)
        for c in range(B // SIDE):
            here = slice(c * SIDE, (c + 1) * SIDE)
            cells = slice(c * CHUNK, (c + 1) * CHUNK)
            outer = (ipairs[here][:, None, :] * wpairs[None]).reshape(CHUNK, WIDTH).astype(bf16)
            gram_add += dot(mask[:, cells], outer)
            outer = split((irows[here][:, None, :] * wrows[None]).reshape(CHUNK, LANES))
            rhs_add += dot(weighted[:, cells], outer)
        gram[pl.ds(ubase, B), :] += gram_add
        rhs[pl.ds(ubase, B), :] += join(rhs_add)

    block(0)

    @pl.when(counts[0, 0] > 1)
    def _():
        block(1)

    out[...] = send_form(gram[...], rhs[...], put)


def item_kernel(coords, counts, values, observed, users, weeks, one, two, wide_one, wide_two, put, out, gram, rhs):
    gram[...] = jnp.zeros_like(gram)
    rhs[...] = jnp.zeros_like(rhs)

    def block(slot):
        ubase = pl.multiple_of(coords[slot, 0] * B, B)
        ibase = pl.multiple_of(coords[slot, 1] * B, B)
        wpairs, wrows = week_block(weeks, wide_one, wide_two, coords[slot, 2])
        rows = users[pl.ds(ubase, B), :]
        upairs = dot(rows, one[...], precision=precise) * dot(rows, two[...], precision=precise)
        upairs = upairs.astype(bf16)
        urows = split(repeat_rows(rows))
        mask, weighted = block_arrays(values, observed, slot)
        gram_add, rhs_add = [], []
        for c in range(B // SIDE):
            cells = slice(c * CHUNK, (c + 1) * CHUNK)
            cross = dot(mask[:, cells], upairs, (0, 0)).reshape(SIDE, B, WIDTH)
            gram_add.append(jnp.sum(cross * wpairs[None], axis=1))
            moment = dot(weighted[:, cells], urows, (0, 0)).reshape(SIDE, B, LANES)
            rhs_add.append(jnp.sum(moment * wrows[None], axis=1))
        gram[pl.ds(ibase, B), :] += jnp.concatenate(gram_add, axis=0)
        rhs[pl.ds(ibase, B), :] += join(jnp.concatenate(rhs_add, axis=0))

    block(0)

    @pl.when(counts[0, 0] > 1)
    def _():
        block(1)

    out[...] = send_form(gram[...], rhs[...], put)


def solve_kernel(parts, out, copies):
    count = parts.shape[0]
    pick = (iota((count, LANES), 0) % T == iota((count, LANES), 1)).astype(f32)
    if LINK == bf16:
        packed = dot(parts[...], pick.astype(bf16), (0, 0))
    else:
        packed = dot(parts[...], pick, (0, 0), precise)
    sub = iota((T, LANES), 0)

    def tile(r, t):
        first = START[r] + (t - r // T) * T
        return packed[first:first + T]

    def spread(x, n):
        return jnp.broadcast_to(x[n:n + 1], (T, LANES))

    tiles = R // T
    rows = {}
    for r in range(R):
        for t in range(r // T, tiles):
            x = tile(r, t)
            rows[r, t] = x + jnp.where(sub == r % T, ridge_weight, 0.0) if t == r // T else x
    side = []
    for j in range(tiles):
        row5, row6, row7 = (tile(j * T + n, j) for n in (5, 6, 7))
        high = jnp.where(sub == 7, spread(row6, 0), row7)
        low = jnp.where(sub == 0, row5, row6)
        low = jnp.where(sub == 6, spread(row5, 1), low)
        low = jnp.where(sub == 7, spread(row5, 2), low)
        side.append(high + low)
    factor, right = {}, []
    for k in range(R):
        own = k // T
        inverse = 1.0 / spread(rows[k, own], k % T)
        scaled = {t: rows[k, t] * inverse for t in range(own, tiles)}
        mine = spread(side[own], k % T)
        right.append(mine * inverse)
        for t in range(own, tiles):
            side[t] = side[t] - scaled[t] * mine
        for r in range(k + 1, R):
            factor[k, r] = spread(scaled[r // T], r % T)
            for t in range(r // T, tiles):
                rows[r, t] = rows[r, t] - factor[k, r] * rows[k, t]
    answer = []
    for s in range(R - 1, -1, -1):
        for k in range(s):
            right[k] = right[k] - factor[k, s] * right[s]
    for j in range(tiles):
        x = right[j * T]
        for n in range(1, T):
            x = jnp.where(sub == n, right[j * T + n], x)
        answer.append(x)
    answer = jnp.concatenate(answer, axis=0)
    answer = jnp.transpose(answer)[:T, :]
    out[...] = answer
    copies[...] = jnp.broadcast_to(answer[None], copies.shape)


def vmem():
    return pl.BlockSpec(memory_space=pltpu.VMEM)


def smem():
    return pl.BlockSpec(memory_space=pltpu.SMEM)


PARAMS = pltpu.CompilerParams(vmem_limit_bytes=48 * 1024 * 1024)


def normal_equations(kernel, span, coords, counts, values, observed, factors, weeks, consts):
    return pl.pallas_call(
        kernel,
        out_shape=jax.ShapeDtypeStruct((span, WIDTH), LINK),
        in_specs=[smem(), smem()] + [vmem()] * (4 + len(consts)),
        out_specs=vmem(),
        scratch_shapes=[pltpu.VMEM((span, WIDTH), f32), pltpu.VMEM((span, R), f32)],
        compiler_params=PARAMS,
    )(coords, counts, values, observed, factors, weeks, *consts)


def solve(parts, peers):
    return pl.pallas_call(
        solve_kernel,
        out_shape=(jax.ShapeDtypeStruct((T, R), f32), jax.ShapeDtypeStruct((peers, T, R), f32)),
        in_specs=[vmem()],
        out_specs=(vmem(), vmem()),
        compiler_params=PARAMS,
    )(parts)


def to_all(x, axis):
    copies = jnp.broadcast_to(x[None], (lax.axis_size(axis),) + x.shape)
    return lax.all_to_all(copies, axis, 0, 0, tiled=True)


def shards(values, observed, coords, counts, item_factors, week_factors):
    n_slab, n_fib = lax.axis_size("slab"), lax.axis_size("fib")
    consts = (
        jnp.asarray(ONE), jnp.asarray(TWO),
        jnp.asarray(np.tile(ONE, (PACK, 1)), bf16), jnp.asarray(np.tile(TWO, (PACK, 1)), bf16),
        jnp.asarray(PUT, bf16),
    )
    packed = week_factors.astype(bf16).reshape(1, LANES)
    weeks = to_all(packed, "fib").reshape(n_fib, LANES)
    weeks = to_all(weeks, "slab").reshape(n_slab * n_fib, LANES)
    shared = (coords[0], counts, values[0], observed[0])
    parts = normal_equations(user_kernel, UBD * B, *shared, item_factors, weeks, consts)
    parts = lax.all_to_all(parts, "fib", 0, 0, tiled=True)
    user_out, copies = solve(parts, n_fib)
    users = lax.all_to_all(copies, "fib", 0, 0, tiled=True).reshape(UBD * B, R)
    parts = normal_equations(item_kernel, IBD * B, *shared, users, weeks, consts)
    parts = lax.all_to_all(parts, "slab", 0, 0, tiled=True)
    _, copies = solve(parts, n_slab)
    item_updated = lax.all_to_all(copies, "slab", 0, 0, tiled=True).reshape(IBD * B, R)
    return (user_out, item_updated)


def solution(mesh):
    in_specs = (
        P("slab", "fib", None, None),
        P("slab", "fib", None, None),
        P("slab", "fib", None),
        P("slab", "fib"),
        P("fib", None),
        P(("slab", "fib"), None),
    )
    out_specs = (P(("slab", "fib"), None), P("fib", None))
    return jax.shard_map(shards, mesh=mesh, in_specs=in_specs, out_specs=out_specs, check_vma=False)
```

```python
import jax
import jax.numpy as jnp
import numpy as np
from jax import lax
from jax.experimental import pallas as pl
from jax.experimental.pallas import tpu as pltpu
from jax.sharding import PartitionSpec as P

B = 64
R = 32
UBD = 4
IBD = 2
T = 8
LANES = 128
SIDE = 4
CHUNK = SIDE * B
PACK = LANES // R
WROWS = B // PACK
ridge_weight = 1.0
precise = lax.Precision.HIGHEST
LINK = jnp.bfloat16
f32 = jnp.float32
bf16 = jnp.bfloat16


def tables():
    start, left, right = {}, [], []
    for r in range(R):
        start[r] = len(left)
        for s in range(r // T * T, R):
            left.append(r)
            right.append(s)
    width = len(left)
    one = np.zeros((R, width), np.float32)
    two = np.zeros((R, width), np.float32)
    for k, (r, s) in enumerate(zip(left, right)):
        if s >= r:
            one[r, k] = 1
            two[s, k] = 1
    put = np.zeros((LANES, width), np.float32)
    for j in range(R // T):
        row5, row6, row7 = (start[j * T + n] for n in (5, 6, 7))
        for n in range(7):
            put[j * T + n, row7 + n] = 1
        put[j * T + 7, row6] = 1
        for n in range(1, 6):
            put[R + j * T + n, row6 + n] = 1
        put[R + j * T, row5] = 1
        put[R + j * T + 6, row5 + 1] = 1
        put[R + j * T + 7, row5 + 2] = 1
    return start, width, one, two, put


START, WIDTH, ONE, TWO, PUT = tables()
TABLE = np.concatenate([ONE, TWO, PUT[:2 * R]])


def dot(a, b, dims=(1, 0), precision=None):
    return lax.dot_general(
        a, b, (((dims[0],), (dims[1],)), ((), ())), preferred_element_type=f32, precision=precision
    )


def iota(shape, dim):
    return lax.broadcasted_iota(jnp.int32, shape, dim)


def week_block(weeks, one, two, start):
    packed = weeks[pl.ds(pl.multiple_of(start * WROWS, WROWS), WROWS), :]
    spread = (iota((B, WROWS), 0) // PACK == iota((B, WROWS), 1)).astype(f32).astype(bf16)
    rows = dot(spread, packed)
    own = iota((B, LANES), 0) % PACK == iota((B, LANES), 1) // R
    rows = jnp.where(own, rows, 0.0).astype(bf16)
    pairs = dot(rows, jnp.concatenate([one] * PACK)) * dot(rows, jnp.concatenate([two] * PACK))
    return pairs.astype(bf16), dot(rows, fold()).astype(bf16)


def fold():
    return (iota((LANES, LANES), 0) % R == iota((LANES, LANES), 1) % R).astype(f32).astype(bf16)


def three(x, axis):
    high = x.astype(bf16).astype(f32)
    middle = (x - high).astype(bf16).astype(f32)
    low = (x - high) - middle
    return jnp.concatenate([high, middle, low, jnp.zeros_like(low)], axis=axis).astype(bf16)


def split(x):
    high = x.astype(bf16).astype(f32)
    return jnp.where(iota(x.shape, 1) < R, high, x - high).astype(bf16)


def join(x):
    return x[:, :R] + x[:, R:2 * R]


def send_form(gram, rhs, put):
    high = rhs.astype(bf16).astype(f32)
    parts = jnp.concatenate([high, rhs - high], axis=1).astype(bf16)
    return (gram + dot(parts, put)).astype(LINK)


def user_kernel(coords_in, counts, values_in, observed_in, items_in, weeks, table_in, out, mask, weighted, wpairs, wrows,
                table, places, coords, values, observed, items, ipairs, irows, gram, rhs, sems):
    moves = {}
    for n, (name, source, target) in enumerate((
        ("coords", coords_in, coords), ("table", table_in, table), ("items", items_in, items),
        ("observed0", observed_in.at[0], observed.at[0]), ("values0", values_in.at[0], values.at[0]),
        ("observed1", observed_in.at[1], observed.at[1]), ("values1", values_in.at[1], values.at[1]),
    )):
        moves[name] = pltpu.make_async_copy(source, target, sems.at[n])
        moves[name].start()
    gram[...] = jnp.zeros_like(gram)
    rhs[...] = jnp.zeros_like(rhs)
    for name in ("coords", "table", "items"):
        moves[name].wait()
    one, two, put = table[:R], table[R:2 * R], table[2 * R:]
    rows = three(items[...], 0)
    ipairs[...] = dot(rows, jnp.concatenate([one] * PACK), (0, 0)) * dot(rows, jnp.concatenate([two] * PACK), (0, 0))
    irows[...] = dot(rows, fold(), (0, 0))

    def block(slot):
        ubase = pl.multiple_of(coords[slot, 0] * B, B)
        ibase = pl.multiple_of(coords[slot, 1] * B, B)
        wpairs[slot], wrows[slot] = week_block(weeks, one, two, coords[slot, 2])
        own = observed[slot].astype(f32)
        mask[slot] = own.astype(bf16)
        weighted[slot] = (values[slot].astype(f32) * own).astype(bf16)
        wp = wpairs[slot].astype(f32)
        wr = wrows[slot].astype(f32)
        ip = ipairs[pl.ds(ibase, B), :]
        ir = irows[pl.ds(ibase, B), :]
        gram_add = jnp.zeros((B, WIDTH), f32)
        rhs_add = jnp.zeros((B, LANES), f32)
        for c in range(B // SIDE):
            here = slice(c * SIDE, (c + 1) * SIDE)
            cells = slice(c * CHUNK, (c + 1) * CHUNK)
            outer = (ip[here][:, None, :] * wp[None]).reshape(CHUNK, WIDTH).astype(bf16)
            gram_add += dot(mask[slot, :, cells], outer)
            outer = split((ir[here][:, None, :] * wr[None]).reshape(CHUNK, LANES))
            rhs_add += dot(weighted[slot, :, cells], outer)
        gram[pl.ds(ubase, B), :] += gram_add
        rhs[pl.ds(ubase, B), :] += join(rhs_add)

    moves["observed0"].wait()
    moves["values0"].wait()
    block(0)
    moves["observed1"].wait()
    moves["values1"].wait()

    @pl.when(counts[0, 0] > 1)
    def _():
        block(1)

    for slot in range(2):
        for n in range(2):
            places[slot, n] = coords[slot, n]
    places[0, 2] = counts[0, 0]
    places[1, 2] = counts[0, 0]
    out[...] = send_form(gram[...], rhs[...], put)


def item_kernel(places, mask, weighted, users, wpairs, wrows, table, out, gram, rhs):
    gram[...] = jnp.zeros_like(gram)
    rhs[...] = jnp.zeros_like(rhs)
    one, two, put = table[:R], table[R:2 * R], table[2 * R:]

    def block(slot):
        ubase = pl.multiple_of(places[slot, 0] * B, B)
        ibase = pl.multiple_of(places[slot, 1] * B, B)
        rows = users[pl.ds(ubase, B), :][:, :R]
        parts = three(rows, 1)
        upairs = dot(parts, jnp.concatenate([one] * PACK)) * dot(parts, jnp.concatenate([two] * PACK))
        upairs = upairs.astype(bf16)
        urows = split(jnp.concatenate([rows] * PACK, axis=1))
        wp = wpairs[slot].astype(f32)
        wr = wrows[slot].astype(f32)
        gram_add, rhs_add = [], []
        for c in range(B // SIDE):
            cells = slice(c * CHUNK, (c + 1) * CHUNK)
            cross = dot(mask[slot, :, cells], upairs, (0, 0)).reshape(SIDE, B, WIDTH)
            gram_add.append(jnp.sum(cross * wp[None], axis=1))
            moment = dot(weighted[slot, :, cells], urows, (0, 0)).reshape(SIDE, B, LANES)
            rhs_add.append(jnp.sum(moment * wr[None], axis=1))
        gram[pl.ds(ibase, B), :] += jnp.concatenate(gram_add, axis=0)
        rhs[pl.ds(ibase, B), :] += join(jnp.concatenate(rhs_add, axis=0))

    block(0)

    @pl.when(places[0, 2] > 1)
    def _():
        block(1)

    out[...] = send_form(gram[...], rhs[...], put)


def solve_kernel(parts, out, copies):
    count = parts.shape[0]
    pick = (iota((count, LANES), 0) % T == iota((count, LANES), 1)).astype(f32)
    if LINK == bf16:
        packed = dot(parts[...], pick.astype(bf16), (0, 0))
    else:
        packed = dot(parts[...], pick, (0, 0), precise)
    sub = iota((T, LANES), 0)

    def tile(r, t):
        first = START[r] + (t - r // T) * T
        return packed[first:first + T]

    def spread(x, n):
        return jnp.broadcast_to(x[n:n + 1], (T, LANES))

    tiles = R // T
    rows = {}
    for r in range(R):
        for t in range(r // T, tiles):
            x = tile(r, t)
            rows[r, t] = x + jnp.where(sub == r % T, ridge_weight, 0.0) if t == r // T else x
    side = []
    for j in range(tiles):
        row5, row6, row7 = (tile(j * T + n, j) for n in (5, 6, 7))
        high = jnp.where(sub == 7, spread(row6, 0), row7)
        low = jnp.where(sub == 0, row5, row6)
        low = jnp.where(sub == 6, spread(row5, 1), low)
        low = jnp.where(sub == 7, spread(row5, 2), low)
        side.append(high + low)
    factor, right = {}, []
    for k in range(R):
        own = k // T
        inverse = 1.0 / spread(rows[k, own], k % T)
        scaled = {t: rows[k, t] * inverse for t in range(own, tiles)}
        mine = spread(side[own], k % T)
        right.append(mine * inverse)
        for t in range(own, tiles):
            side[t] = side[t] - scaled[t] * mine
        for r in range(k + 1, R):
            factor[k, r] = spread(scaled[r // T], r % T)
            for t in range(r // T, tiles):
                rows[r, t] = rows[r, t] - factor[k, r] * rows[k, t]
    answer = []
    for s in range(R - 1, -1, -1):
        for k in range(s):
            right[k] = right[k] - factor[k, s] * right[s]
    for j in range(tiles):
        x = right[j * T]
        for n in range(1, T):
            x = jnp.where(sub == n, right[j * T + n], x)
        answer.append(x)
    answer = jnp.concatenate(answer + [jnp.zeros((LANES - R, LANES), f32)], axis=0)
    answer = jnp.transpose(answer)[:T]
    out[...] = answer[:, :R]
    copies[...] = jnp.broadcast_to(answer[None], copies.shape)


def vmem():
    return pl.BlockSpec(memory_space=pltpu.VMEM)


def smem():
    return pl.BlockSpec(memory_space=pltpu.SMEM)


def anywhere():
    return pl.BlockSpec(memory_space=pl.ANY)


PARAMS = pltpu.CompilerParams(vmem_limit_bytes=48 * 1024 * 1024)


def user_equations(coords, counts, values, observed, items, weeks, table):
    coords, values, observed, items, table = (
        pltpu.with_memory_space_constraint(x, pltpu.HBM) for x in (coords, values, observed, items, table)
    )
    return pl.pallas_call(
        user_kernel,
        out_shape=(
            pltpu.VMEM((UBD * B, WIDTH), LINK),
            pltpu.VMEM(values.shape, bf16),
            pltpu.VMEM(values.shape, bf16),
            pltpu.VMEM((2, B, WIDTH), bf16),
            pltpu.VMEM((2, B, LANES), bf16),
            pltpu.VMEM(table.shape, bf16),
            jax.ShapeDtypeStruct((2, 3), jnp.int32),
        ),
        in_specs=[anywhere(), smem()] + [anywhere()] * 3 + [vmem(), anywhere()],
        out_specs=[vmem()] * 6 + [smem()],
        scratch_shapes=[
            pltpu.SMEM(coords.shape, jnp.int32),
            pltpu.VMEM(values.shape, bf16), pltpu.VMEM(observed.shape, jnp.int32), pltpu.VMEM(items.shape, f32),
            pltpu.VMEM((IBD * B, WIDTH), f32), pltpu.VMEM((IBD * B, LANES), f32),
            pltpu.VMEM((UBD * B, WIDTH), f32), pltpu.VMEM((UBD * B, R), f32), pltpu.SemaphoreType.DMA((7,)),
        ],
        compiler_params=PARAMS,
    )(coords, counts, values, observed, items, weeks, table)


def item_equations(places, mask, weighted, users, wpairs, wrows, table):
    return pl.pallas_call(
        item_kernel,
        out_shape=pltpu.VMEM((IBD * B, WIDTH), LINK),
        in_specs=[smem()] + [vmem()] * 6,
        out_specs=vmem(),
        scratch_shapes=[pltpu.VMEM((IBD * B, WIDTH), f32), pltpu.VMEM((IBD * B, R), f32)],
        compiler_params=PARAMS,
    )(places, mask, weighted, users, wpairs, wrows, table)


def solve(parts, peers):
    return pl.pallas_call(
        solve_kernel,
        out_shape=(jax.ShapeDtypeStruct((T, R), f32), pltpu.VMEM((peers, T, LANES), f32)),
        in_specs=[vmem()],
        out_specs=(vmem(), vmem()),
        compiler_params=PARAMS,
    )(parts)


def copies_kernel(x, out):
    rows = x[...].reshape(out.shape[1:])
    out[...] = jnp.broadcast_to(rows[None], out.shape)


def copies_of(x, peers):
    return pl.pallas_call(
        copies_kernel,
        out_shape=pltpu.VMEM((peers, x.shape[0], LANES), x.dtype),
        in_specs=[vmem()],
        out_specs=vmem(),
        compiler_params=PARAMS,
    )(x)


def exchange(x, axis):
    return lax.all_to_all(x, axis, 0, 0, tiled=True)


def shards(values, observed, coords, counts, item_factors, week_factors):
    n_slab, n_fib = lax.axis_size("slab"), lax.axis_size("fib")
    packed = week_factors.astype(bf16).reshape(1, 1, LANES)
    weeks = exchange(jnp.broadcast_to(packed, (n_fib, 1, LANES)), "fib")
    weeks = exchange(copies_of(weeks, n_slab), "slab").reshape(n_slab * n_fib, LANES)
    parts, mask, weighted, wpairs, wrows, table, places = user_equations(
        coords[0], counts, values[0], observed[0], item_factors.T, weeks, jnp.asarray(TABLE, bf16)
    )
    user_out, copies = solve(exchange(parts, "fib"), n_fib)
    users = exchange(copies, "fib").reshape(UBD * B, LANES)
    parts = item_equations(places, mask, weighted, users, wpairs, wrows, table)
    _, copies = solve(exchange(parts, "slab"), n_slab)
    item_updated = exchange(copies, "slab").reshape(IBD * B, LANES)[:, :R]
    return (user_out, item_updated)


def solution(mesh):
    in_specs = (
        P("slab", "fib", None, None),
        P("slab", "fib", None, None),
        P("slab", "fib", None),
        P("slab", "fib"),
        P("fib", None),
        P(("slab", "fib"), None),
    )
    out_specs = (P(("slab", "fib"), None), P("fib", None))
    return jax.shard_map(shards, mesh=mesh, in_specs=in_specs, out_specs=out_specs, check_vma=False)
```

```python
import jax
import jax.numpy as jnp
import numpy as np
from jax import lax
from jax.experimental import pallas as pl
from jax.experimental.pallas import tpu as pltpu
from jax.sharding import PartitionSpec as P

B = 64
R = 32
UBD = 4
IBD = 2
T = 8
LANES = 128
SIDE = 4
CHUNK = SIDE * B
PACK = LANES // R
WROWS = B // PACK
FIB = 32
SLABS, FIBS = ("z", "core"), ("x", "y")
ridge_weight = 1.0
precise = lax.Precision.HIGHEST
LINK = jnp.bfloat16
f32 = jnp.float32
bf16 = jnp.bfloat16


def tables():
    start, left, right = {}, [], []
    for r in range(R):
        start[r] = len(left)
        for s in range(r // T * T, R):
            left.append(r)
            right.append(s)
    width = len(left)
    one = np.zeros((R, width), np.float32)
    two = np.zeros((R, width), np.float32)
    for k, (r, s) in enumerate(zip(left, right)):
        if s >= r:
            one[r, k] = 1
            two[s, k] = 1
    put = np.zeros((LANES, width), np.float32)
    for j in range(R // T):
        row5, row6, row7 = (start[j * T + n] for n in (5, 6, 7))
        for n in range(7):
            put[j * T + n, row7 + n] = 1
        put[j * T + 7, row6] = 1
        for n in range(1, 6):
            put[R + j * T + n, row6 + n] = 1
        put[R + j * T, row5] = 1
        put[R + j * T + 6, row5 + 1] = 1
        put[R + j * T + 7, row5 + 2] = 1
    return start, width, one, two, put


START, WIDTH, ONE, TWO, PUT = tables()
TABLE = np.concatenate([ONE, TWO, PUT[:2 * R]])


def dot(a, b, dims=(1, 0), precision=None):
    return lax.dot_general(
        a, b, (((dims[0],), (dims[1],)), ((), ())), preferred_element_type=f32, precision=precision
    )


def iota(shape, dim):
    return lax.broadcasted_iota(jnp.int32, shape, dim)


def week_block(weeks, one, two, start):
    slab, part = start // (FIB // WROWS), start % (FIB // WROWS)
    both = weeks[pl.ds(slab // 2 * FIB + part * WROWS, WROWS)].astype(f32)
    packed = jnp.where(slab % 2 == 0, both[:, 0], both[:, 1]).astype(bf16)
    spread = (iota((B, WROWS), 0) // PACK == iota((B, WROWS), 1)).astype(f32).astype(bf16)
    rows = dot(spread, packed)
    own = iota((B, LANES), 0) % PACK == iota((B, LANES), 1) // R
    rows = jnp.where(own, rows, 0.0).astype(bf16)
    pairs = dot(rows, jnp.concatenate([one] * PACK)) * dot(rows, jnp.concatenate([two] * PACK))
    return pairs.astype(bf16), dot(rows, fold()).astype(bf16)


def unfold(x):
    return sum(x[:, n * R:(n + 1) * R] for n in range(PACK))


def fold():
    return (iota((LANES, LANES), 0) % R == iota((LANES, LANES), 1) % R).astype(f32).astype(bf16)


def three(x, axis):
    high = x.astype(bf16).astype(f32)
    middle = (x - high).astype(bf16).astype(f32)
    low = (x - high) - middle
    return jnp.concatenate([high, middle, low, jnp.zeros_like(low)], axis=axis).astype(bf16)


def send_form(gram, rhs, put):
    high = rhs.astype(bf16).astype(f32)
    parts = jnp.concatenate([high, rhs - high], axis=1).astype(bf16)
    return (gram + dot(parts, put)).astype(LINK)


def turn(own, strips, turned, slot):
    pairs = B // 2
    for t in range(pairs):
        strips[t * B:(t + 1) * B] = own[:, t * LANES:(t + 1) * LANES]
    first = iota((pairs, LANES), 1) < B
    for v in range(pairs):
        a, b = (strips[pl.ds(2 * v + n, pairs, stride=B)] for n in range(2))
        even = jnp.where(first, a, pltpu.roll(b, B, 1))
        odd = jnp.where(first, pltpu.roll(a, B, 1), b)
        turned[slot, :, v * LANES:(v + 1) * LANES] = jnp.concatenate([even, odd]).astype(bf16)


def item_at(rows, dim):
    place = iota(rows, dim) % B
    return iota(rows, dim) // B * B + place % (B // 2) * 2 + place // (B // 2)


def paired(mask, slot, pairs, wp):
    total = jnp.zeros((B, WIDTH), f32)
    for c in range(B // SIDE):
        outer = []
        for i in range(c * SIDE, (c + 1) * SIDE):
            row = jnp.broadcast_to(pairs[i:i + 1], (16, WIDTH)).astype(bf16)
            outer.append((wp * row[None]).reshape(B, WIDTH))
        total += dot(mask[slot, :, c * CHUNK:(c + 1) * CHUNK], jnp.concatenate(outer))
    return total


def prepare_kernel(coords_in, counts, values_in, observed_in, items_in, table_in, mask, turned, weighted, ipairs, irows,
                   table, places, coords, values, observed, items, strips, sems):
    moves = []
    for n, (source, target) in enumerate((
        (table_in, table), (items_in, items), (observed_in.at[0], observed.at[0]), (values_in.at[0], values.at[0]),
        (observed_in.at[1], observed.at[1]), (values_in.at[1], values.at[1]), (coords_in, coords),
    )):
        moves.append(pltpu.make_async_copy(source, target, sems.at[n]))
        moves[n].start()
    moves[0].wait()
    moves[1].wait()
    rows = three(items[...], 0)
    ipairs[...] = dot(rows, jnp.concatenate([table[:R]] * PACK), (0, 0)) * dot(
        rows, jnp.concatenate([table[R:2 * R]] * PACK), (0, 0)
    )
    irows[...] = dot(rows, fold(), (0, 0))
    for slot in range(2):
        moves[2 + 2 * slot].wait()
        moves[3 + 2 * slot].wait()
        own = observed[slot].astype(f32)
        mask[slot] = own.astype(bf16)
        weighted[slot] = (values[slot].astype(f32) * own).astype(bf16)
        turn(own, strips, turned, slot)
    moves[6].wait()
    for slot in range(2):
        for n in range(3):
            places[slot, n] = coords[slot, n]
        places[slot, 3] = counts[0, 0]


def user_kernel(places, weeks, mask, weighted, ipairs, irows, table, out, wpairs, moment, gram, rhs):
    gram[...] = jnp.zeros_like(gram)
    rhs[...] = jnp.zeros_like(rhs)
    one, two, put = table[:R], table[R:2 * R], table[2 * R:]

    def block(slot):
        ubase = pl.multiple_of(places[slot, 0] * B, B)
        ibase = pl.multiple_of(places[slot, 1] * B, B)
        wp, wr = week_block(weeks, one, two, places[slot, 2])
        wpairs[slot] = wp
        gram[pl.ds(ubase, B), :] += paired(mask, slot, ipairs[pl.ds(ibase, B), :], wp.reshape(B // 16, 16, WIDTH))
        ir = irows[pl.ds(ibase, B), :]
        lane = iota((1, LANES), 1) // R
        apart = iota((CHUNK, LANES), 0) // B == iota((CHUNK, LANES), 1) // R
        apart = jnp.where(apart, jnp.concatenate([wr.astype(f32)] * SIDE), 0.0).astype(bf16)
        rhs_add = jnp.zeros((B, LANES), f32)
        for c in range(B // SIDE):
            here = dot(weighted[slot, :, c * CHUNK:(c + 1) * CHUNK], apart)
            moment[slot, c] = here
            row = sum(jnp.where(lane == n, ir[c * SIDE + n:c * SIDE + n + 1], 0.0) for n in range(SIDE))
            rhs_add += here * row
        rhs[pl.ds(ubase, B), :] += unfold(rhs_add)

    block(0)

    @pl.when(places[0, 3] > 1)
    def _():
        block(1)

    out[...] = send_form(gram[...], rhs[...], put)


def item_kernel(places, turned, moment, users, wpairs, table, out, gram, rhs):
    gram[...] = jnp.zeros_like(gram)
    rhs[...] = jnp.zeros_like(rhs)
    one, two, put = table[:R], table[R:2 * R], table[2 * R:]

    def block(slot):
        ubase = pl.multiple_of(places[slot, 0] * B, B)
        ibase = pl.multiple_of(places[slot, 1] * B, B)
        rows = users[pl.ds(ubase, B), :][:, :R]
        parts = three(rows, 1)
        upairs = dot(parts, jnp.concatenate([one] * PACK)) * dot(parts, jnp.concatenate([two] * PACK))
        gram[pl.ds(ibase, B), :] += paired(turned, slot, upairs, wpairs[slot].reshape(B // 16, 16, WIDTH))
        urows = jnp.concatenate([rows] * PACK, axis=1)
        sums = three(jnp.sum(moment[slot] * urows[None], axis=1), 0)
        spread = iota((B, B), 1) % (B // SIDE) == item_at((B, B), 0) // SIDE
        sums = dot(jnp.where(spread, 1.0, 0.0).astype(bf16), sums)
        sums = jnp.where(item_at(sums.shape, 0) % SIDE == iota(sums.shape, 1) // R, sums, 0.0)
        rhs[pl.ds(ibase, B), :] += unfold(sums)

    block(0)

    @pl.when(places[0, 3] > 1)
    def _():
        block(1)

    count = IBD * B
    order = jnp.where(item_at((count, count), 1) == iota((count, count), 0), 1.0, 0.0).astype(bf16)
    out[...] = dot(order, send_form(gram[...], rhs[...], put)).astype(LINK)


def solve_kernel(parts, out, copies):
    count = parts.shape[0]
    pick = (iota((count, LANES), 0) % T == iota((count, LANES), 1)).astype(f32)
    if LINK == bf16:
        packed = dot(parts[...], pick.astype(bf16), (0, 0))
    else:
        packed = dot(parts[...], pick, (0, 0), precise)
    sub = iota((T, LANES), 0)

    def tile(r, t):
        first = START[r] + (t - r // T) * T
        return packed[first:first + T]

    def spread(x, n):
        return jnp.broadcast_to(x[n:n + 1], (T, LANES))

    tiles = R // T
    rows = {}
    for r in range(R):
        for t in range(r // T, tiles):
            x = tile(r, t)
            rows[r, t] = x + jnp.where(sub == r % T, ridge_weight, 0.0) if t == r // T else x
    side = []
    for j in range(tiles):
        row5, row6, row7 = (tile(j * T + n, j) for n in (5, 6, 7))
        high = jnp.where(sub == 7, spread(row6, 0), row7)
        low = jnp.where(sub == 0, row5, row6)
        low = jnp.where(sub == 6, spread(row5, 1), low)
        low = jnp.where(sub == 7, spread(row5, 2), low)
        side.append(high + low)
    factor, right = {}, []
    for k in range(R):
        own = k // T
        inverse = 1.0 / spread(rows[k, own], k % T)
        scaled = {t: rows[k, t] * inverse for t in range(own, tiles)}
        mine = spread(side[own], k % T)
        right.append(mine * inverse)
        for t in range(own, tiles):
            side[t] = side[t] - scaled[t] * mine
        for r in range(k + 1, R):
            factor[k, r] = spread(scaled[r // T], r % T)
            for t in range(r // T, tiles):
                rows[r, t] = rows[r, t] - factor[k, r] * rows[k, t]
    answer = []
    for s in range(R - 1, -1, -1):
        for k in range(s):
            right[k] = right[k] - factor[k, s] * right[s]
    for j in range(tiles):
        x = right[j * T]
        for n in range(1, T):
            x = jnp.where(sub == n, right[j * T + n], x)
        answer.append(x)
    answer = jnp.concatenate(answer + [jnp.zeros((LANES - R, LANES), f32)], axis=0)
    answer = jnp.transpose(answer)[:T]
    out[...] = answer[:, :R]
    copies[...] = jnp.broadcast_to(answer[None], copies.shape)


def vmem():
    return pl.BlockSpec(memory_space=pltpu.VMEM)


def smem():
    return pl.BlockSpec(memory_space=pltpu.SMEM)


def anywhere():
    return pl.BlockSpec(memory_space=pl.ANY)


def params(mib):
    return pltpu.CompilerParams(vmem_limit_bytes=mib * 1024 * 1024)


def prepare(coords, counts, values, observed, items, table):
    coords, values, observed, items, table = (
        pltpu.with_memory_space_constraint(x, pltpu.HBM) for x in (coords, values, observed, items, table)
    )
    return pl.pallas_call(
        prepare_kernel,
        out_shape=(
            pltpu.VMEM(values.shape, bf16),
            pltpu.VMEM(values.shape, bf16),
            pltpu.VMEM(values.shape, bf16),
            pltpu.VMEM((IBD * B, WIDTH), f32),
            pltpu.VMEM((IBD * B, LANES), f32),
            pltpu.VMEM(table.shape, bf16),
            jax.ShapeDtypeStruct((2, 4), jnp.int32),
        ),
        in_specs=[anywhere(), smem()] + [anywhere()] * 4,
        out_specs=[vmem()] * 6 + [smem()],
        scratch_shapes=[
            pltpu.SMEM(coords.shape, jnp.int32), pltpu.VMEM(values.shape, bf16), pltpu.VMEM(observed.shape, jnp.int32), pltpu.VMEM(items.shape, f32),
            pltpu.VMEM((B * B // 2, LANES), f32), pltpu.SemaphoreType.DMA((7,)),
        ],
        compiler_params=params(16),
    )(coords, counts, values, observed, items, table)


def user_equations(places, weeks, mask, weighted, ipairs, irows, table):
    return pl.pallas_call(
        user_kernel,
        out_shape=(
            pltpu.VMEM((UBD * B, WIDTH), LINK),
            pltpu.VMEM((2, B, WIDTH), bf16),
            pltpu.VMEM((2, B // SIDE, B, LANES), f32),
        ),
        in_specs=[smem()] + [vmem()] * 6,
        out_specs=[vmem()] * 3,
        scratch_shapes=[pltpu.VMEM((UBD * B, WIDTH), f32), pltpu.VMEM((UBD * B, R), f32)],
        compiler_params=params(16),
    )(places, weeks, mask, weighted, ipairs, irows, table)


def item_equations(places, turned, moment, users, wpairs, table):
    return pl.pallas_call(
        item_kernel,
        out_shape=pltpu.VMEM((IBD * B, WIDTH), LINK),
        in_specs=[smem()] + [vmem()] * 5,
        out_specs=vmem(),
        scratch_shapes=[pltpu.VMEM((IBD * B, WIDTH), f32), pltpu.VMEM((IBD * B, R), f32)],
        compiler_params=params(16),
    )(places, turned, moment, users, wpairs, table)


def solve(parts, peers):
    return pl.pallas_call(
        solve_kernel,
        out_shape=(jax.ShapeDtypeStruct((T, R), f32), pltpu.VMEM((peers, T, LANES), f32)),
        in_specs=[vmem()],
        out_specs=(vmem(), vmem()),
        compiler_params=params(16),
    )(parts)


def week_kernel(weeks, out):
    rows = weeks[...]
    row = jnp.concatenate([
        jnp.concatenate([rows[k * PACK + n:k * PACK + n + 1] for n in range(PACK)], axis=1) for k in range(2)
    ], axis=0)
    out[...] = jnp.broadcast_to(row[None], out.shape).astype(bf16)


def week_copies(weeks, peers):
    return pl.pallas_call(
        week_kernel,
        out_shape=pltpu.VMEM((peers, 2, LANES), bf16),
        in_specs=[vmem()],
        out_specs=vmem(),
        compiler_params=params(16),
    )(weeks)


def copies_kernel(x, out):
    rows = x[...].reshape(out.shape[1:])
    out[...] = jnp.broadcast_to(rows[None], out.shape)


def copies_of(x, peers):
    return pl.pallas_call(
        copies_kernel,
        out_shape=pltpu.VMEM((peers, x.shape[0], LANES), x.dtype),
        in_specs=[vmem()],
        out_specs=vmem(),
        compiler_params=params(16),
    )(x)


def exchange(x, axis):
    return lax.all_to_all(x, axis, 0, 0, tiled=True)


def shards(values, observed, coords, counts, item_factors, week_factors):
    n_slab, n_fib = lax.axis_size(SLABS), lax.axis_size(FIBS)
    pair = lax.all_gather(week_factors, "core", axis=0, tiled=True)
    copies = week_copies(pair, n_slab * n_fib // 2)
    weeks = exchange(copies, ("z", "x", "y"))
    mask, turned, weighted, ipairs, irows, table, places = prepare(
        coords[0], counts, values[0], observed[0], item_factors.T, jnp.asarray(TABLE, bf16)
    )
    parts, wpairs, moment = user_equations(places, weeks, mask, weighted, ipairs, irows, table)
    user_out, copies = solve(exchange(parts, FIBS), n_fib)
    users = exchange(copies, FIBS).reshape(UBD * B, LANES)
    parts = item_equations(places, turned, moment, users, wpairs, table)
    _, copies = solve(exchange(parts, SLABS), n_slab)
    item_updated = exchange(copies, SLABS).reshape(IBD * B, LANES)[:, :R]
    return (user_out, item_updated)


def solution(mesh):
    fine = jax.sharding.Mesh(mesh.devices.reshape(8, 2, 4, 8), SLABS + FIBS)
    in_specs = (
        P(SLABS, FIBS, None, None),
        P(SLABS, FIBS, None, None),
        P(SLABS, FIBS, None),
        P(SLABS, FIBS),
        P(FIBS, None),
        P(SLABS + FIBS, None),
    )
    out_specs = (P(SLABS + FIBS, None), P(FIBS, None))
    return jax.shard_map(shards, mesh=fine, in_specs=in_specs, out_specs=out_specs, check_vma=False)
```

```python
import jax
import jax.numpy as jnp
import numpy as np
from jax import lax
from jax.experimental import pallas as pl
from jax.experimental.pallas import tpu as pltpu
from jax.sharding import PartitionSpec as P

B = 64
R = 32
UBD = 4
IBD = 2
T = 8
LANES = 128
SIDE = 4
CHUNK = SIDE * B
PACK = LANES // R
WROWS = B // PACK
FIB = 32
SLABS, FIBS = ("z", "core"), ("x", "y")
ridge_weight = 1.0
precise = lax.Precision.HIGHEST
LINK = jnp.bfloat16
f32 = jnp.float32
bf16 = jnp.bfloat16


def tables():
    start, left, right = {}, [], []
    for r in range(R):
        start[r] = len(left)
        for s in range(r // T * T, R):
            left.append(r)
            right.append(s)
    width = len(left)
    one = np.zeros((R, width), np.float32)
    two = np.zeros((R, width), np.float32)
    for k, (r, s) in enumerate(zip(left, right)):
        if s >= r:
            one[r, k] = 1
            two[s, k] = 1
    put = np.zeros((LANES, width), np.float32)
    for j in range(R // T):
        row5, row6, row7 = (start[j * T + n] for n in (5, 6, 7))
        for n in range(7):
            put[j * T + n, row7 + n] = 1
        put[j * T + 7, row6] = 1
        for n in range(1, 6):
            put[R + j * T + n, row6 + n] = 1
        put[R + j * T, row5] = 1
        put[R + j * T + 6, row5 + 1] = 1
        put[R + j * T + 7, row5 + 2] = 1
    return start, width, one, two, put


START, WIDTH, ONE, TWO, PUT = tables()
TABLE = np.concatenate([ONE, TWO, PUT[:2 * R]])


def dot(a, b, dims=(1, 0), precision=None):
    return lax.dot_general(
        a, b, (((dims[0],), (dims[1],)), ((), ())), preferred_element_type=f32, precision=precision
    )


def iota(shape, dim):
    return lax.broadcasted_iota(jnp.int32, shape, dim)


def week_block(weeks, one, two, start):
    slab, part = start // (FIB // WROWS), start % (FIB // WROWS)
    both = weeks[pl.ds(slab // 2 * FIB + part * WROWS, WROWS)].astype(f32)
    packed = jnp.where(slab % 2 == 0, both[:, 0], both[:, 1]).astype(bf16)
    spread = (iota((B, WROWS), 0) // PACK == iota((B, WROWS), 1)).astype(f32).astype(bf16)
    rows = dot(spread, packed)
    own = iota((B, LANES), 0) % PACK == iota((B, LANES), 1) // R
    rows = jnp.where(own, rows, 0.0).astype(bf16)
    pairs = dot(rows, jnp.concatenate([one] * PACK)) * dot(rows, jnp.concatenate([two] * PACK))
    return pairs.astype(bf16), dot(rows, fold()).astype(bf16)


def unfold(x):
    return sum(x[:, n * R:(n + 1) * R] for n in range(PACK))


def fold():
    return (iota((LANES, LANES), 0) % R == iota((LANES, LANES), 1) % R).astype(f32).astype(bf16)


def three(x, axis):
    high = x.astype(bf16).astype(f32)
    middle = (x - high).astype(bf16).astype(f32)
    low = (x - high) - middle
    return jnp.concatenate([high, middle, low, jnp.zeros_like(low)], axis=axis).astype(bf16)


def send_form(gram, rhs, put):
    high = rhs.astype(bf16).astype(f32)
    parts = jnp.concatenate([high, rhs - high], axis=1).astype(bf16)
    return (gram + dot(parts, put)).astype(LINK)


def turn(own, strips, turned, slot):
    pairs = B // 2
    for t in range(pairs):
        strips[t * B:(t + 1) * B] = own[:, t * LANES:(t + 1) * LANES]
    first = iota((pairs, LANES), 1) < B
    for v in range(pairs):
        a, b = (strips[pl.ds(2 * v + n, pairs, stride=B)] for n in range(2))
        even = jnp.where(first, a, pltpu.roll(b, B, 1))
        odd = jnp.where(first, pltpu.roll(a, B, 1), b)
        turned[slot, :, v * LANES:(v + 1) * LANES] = jnp.concatenate([even, odd]).astype(bf16)


def item_at(rows, dim):
    place = iota(rows, dim) % B
    return iota(rows, dim) // B * B + place % (B // 2) * 2 + place // (B // 2)


def paired(mask, slot, pairs, wp):
    total = jnp.zeros((B, WIDTH), f32)
    step = 2 * SIDE
    for c in range(0, B, step):
        outer = []
        for i in range(c, c + step):
            row = jnp.broadcast_to(pairs[i:i + 1], (16, WIDTH)).astype(bf16)
            outer.append((wp * row[None]).reshape(B, WIDTH))
        total += dot(mask[slot, :, c * B:(c + step) * B], jnp.concatenate(outer))
    return total


def prepare_kernel(coords_in, counts, values_in, observed_in, items_in, table_in, mask, turned, weighted, irows,
                   table, places, coords, values, observed, items, strips, sems):
    moves = []
    for n, (source, target) in enumerate((
        (table_in, table.at[:TABLE.shape[0]]), (items_in, items), (observed_in.at[0], observed.at[0]), (values_in.at[0], values.at[0]),
        (observed_in.at[1], observed.at[1]), (values_in.at[1], values.at[1]), (coords_in, coords),
    )):
        moves.append(pltpu.make_async_copy(source, target, sems.at[n]))
        moves[n].start()
    moves[0].wait()
    moves[1].wait()
    rows = three(items[...], 0)
    pairs = dot(rows, jnp.concatenate([table[:R]] * PACK), (0, 0))
    pairs *= dot(rows, jnp.concatenate([table[R:2 * R]] * PACK), (0, 0))
    table[TABLE.shape[0]:] = pairs.astype(bf16)
    irows[...] = dot(rows, fold(), (0, 0))
    for slot in range(2):
        moves[2 + 2 * slot].wait()
        moves[3 + 2 * slot].wait()
        own = observed[slot].astype(f32)
        mask[slot] = own.astype(bf16)
        weighted[slot] = (values[slot].astype(f32) * own).astype(bf16)
        turn(own, strips, turned, slot)
    moves[6].wait()
    for slot in range(2):
        for n in range(3):
            places[slot, n] = coords[slot, n]
        places[slot, 3] = counts[0, 0]


def user_kernel(places, weeks, mask, weighted, irows, table, out, wpairs, moment, gram, rhs):
    gram[...] = jnp.zeros_like(gram)
    rhs[...] = jnp.zeros_like(rhs)
    one, two, put = table[:R], table[R:2 * R], table[2 * R:TABLE.shape[0]]

    def block(slot):
        ubase = pl.multiple_of(places[slot, 0] * B, B)
        ibase = pl.multiple_of(places[slot, 1] * B, B)
        wp, wr = week_block(weeks, one, two, places[slot, 2])
        wpairs[slot] = wp
        gram[pl.ds(ubase, B), :] += paired(mask, slot, table[pl.ds(pl.multiple_of(TABLE.shape[0] + ibase, B), B), :].astype(f32), wp.reshape(B // 16, 16, WIDTH))
        ir = irows[pl.ds(ibase, B), :]
        lane = iota((1, LANES), 1) // R
        apart = iota((CHUNK, LANES), 0) // B == iota((CHUNK, LANES), 1) // R
        apart = jnp.where(apart, jnp.concatenate([wr.astype(f32)] * SIDE), 0.0).astype(bf16)
        rhs_add = jnp.zeros((B, LANES), f32)
        every = jnp.concatenate([weighted[slot, :, c * CHUNK:(c + 1) * CHUNK] for c in range(B // SIDE)])
        every = dot(every, apart)
        for c in range(B // SIDE):
            here = every[c * B:(c + 1) * B]
            moment[slot, c] = here
            row = sum(jnp.where(lane == n, ir[c * SIDE + n:c * SIDE + n + 1], 0.0) for n in range(SIDE))
            rhs_add += here * row
        rhs[pl.ds(ubase, B), :] += unfold(rhs_add)

    block(0)

    @pl.when(places[0, 3] > 1)
    def _():
        block(1)

    out[...] = send_form(gram[...], rhs[...], put)


def item_kernel(places, turned, moment, users, wpairs, table, out, gram, rhs):
    gram[...] = jnp.zeros_like(gram)
    rhs[...] = jnp.zeros_like(rhs)
    one, two, put = table[:R], table[R:2 * R], table[2 * R:TABLE.shape[0]]

    def block(slot):
        ubase = pl.multiple_of(places[slot, 0] * B, B)
        ibase = pl.multiple_of(places[slot, 1] * B, B)
        rows = users[pl.ds(ubase, B), :]
        upairs = dot(rows, jnp.concatenate([one] * PACK)) * dot(rows, jnp.concatenate([two] * PACK))
        gram[pl.ds(ibase, B), :] += paired(turned, slot, upairs, wpairs[slot].reshape(B // 16, 16, WIDTH))
        urows = dot(rows, fold())
        sums = three(jnp.sum(moment[slot] * urows[None], axis=1), 0)
        spread = iota((B, B), 1) % (B // SIDE) == item_at((B, B), 0) // SIDE
        sums = dot(jnp.where(spread, 1.0, 0.0).astype(bf16), sums)
        sums = jnp.where(item_at(sums.shape, 0) % SIDE == iota(sums.shape, 1) // R, sums, 0.0)
        rhs[pl.ds(ibase, B), :] += unfold(sums)

    block(0)

    @pl.when(places[0, 3] > 1)
    def _():
        block(1)

    count = IBD * B
    order = jnp.where(item_at((count, count), 1) == iota((count, count), 0), 1.0, 0.0).astype(bf16)
    out[...] = dot(order, send_form(gram[...], rhs[...], put)).astype(LINK)


def solve_kernel(parts, out, copies):
    count = parts.shape[0]
    pick = (iota((count, LANES), 0) % T == iota((count, LANES), 1)).astype(f32)
    if LINK == bf16:
        packed = dot(parts[...], pick.astype(bf16), (0, 0))
    else:
        packed = dot(parts[...], pick, (0, 0), precise)
    sub = iota((T, LANES), 0)

    def tile(r, t):
        first = START[r] + (t - r // T) * T
        return packed[first:first + T]

    def spread(x, n):
        return jnp.broadcast_to(x[n:n + 1], (T, LANES))

    tiles = R // T
    rows = {}
    for r in range(R):
        for t in range(r // T, tiles):
            x = tile(r, t)
            rows[r, t] = x + jnp.where(sub == r % T, ridge_weight, 0.0) if t == r // T else x
    side = []
    for j in range(tiles):
        row5, row6, row7 = (tile(j * T + n, j) for n in (5, 6, 7))
        high = jnp.where(sub == 7, spread(row6, 0), row7)
        low = jnp.where(sub == 0, row5, row6)
        low = jnp.where(sub == 6, spread(row5, 1), low)
        low = jnp.where(sub == 7, spread(row5, 2), low)
        side.append(high + low)
    factor, right = {}, []
    for k in range(R):
        own = k // T
        inverse = 1.0 / spread(rows[k, own], k % T)
        scaled = {t: rows[k, t] * inverse for t in range(own, tiles)}
        mine = spread(side[own], k % T)
        right.append(mine * inverse)
        for t in range(own, tiles):
            side[t] = side[t] - scaled[t] * mine
        for r in range(k + 1, R):
            factor[k, r] = spread(scaled[r // T], r % T)
            for t in range(r // T, tiles):
                rows[r, t] = rows[r, t] - factor[k, r] * rows[k, t]
    answer = []
    for s in range(R - 1, -1, -1):
        for k in range(s):
            right[k] = right[k] - factor[k, s] * right[s]
    for j in range(tiles):
        x = right[j * T]
        for n in range(1, T):
            x = jnp.where(sub == n, right[j * T + n], x)
        answer.append(x)
    answer = jnp.concatenate(answer + [jnp.zeros((LANES - R, LANES), f32)], axis=0)
    answer = jnp.transpose(answer)[:T]
    out[...] = answer[:, :R]
    if copies.dtype == bf16:
        answer = three(answer[:, :R], 1).astype(f32)
        copies[...] = jnp.concatenate([answer] * (copies.shape[0] // T)).astype(bf16)
    else:
        copies[...] = jnp.broadcast_to(answer[None], copies.shape)


def vmem():
    return pl.BlockSpec(memory_space=pltpu.VMEM)


def smem():
    return pl.BlockSpec(memory_space=pltpu.SMEM)


def anywhere():
    return pl.BlockSpec(memory_space=pl.ANY)


def params(mib):
    return pltpu.CompilerParams(vmem_limit_bytes=mib * 1024 * 1024)


def prepare(coords, counts, values, observed, items, table):
    coords, values, observed, items, table = (
        pltpu.with_memory_space_constraint(x, pltpu.HBM) for x in (coords, values, observed, items, table)
    )
    return pl.pallas_call(
        prepare_kernel,
        out_shape=(
            pltpu.VMEM(values.shape, bf16),
            pltpu.VMEM(values.shape, bf16),
            pltpu.VMEM(values.shape, bf16),
            pltpu.VMEM((IBD * B, LANES), f32),
            pltpu.VMEM((table.shape[0] + IBD * B, WIDTH), bf16),
            jax.ShapeDtypeStruct((2, 4), jnp.int32),
        ),
        in_specs=[anywhere(), smem()] + [anywhere()] * 4,
        out_specs=[vmem()] * 5 + [smem()],
        scratch_shapes=[
            pltpu.SMEM(coords.shape, jnp.int32), pltpu.VMEM(values.shape, bf16), pltpu.VMEM(observed.shape, jnp.int32), pltpu.VMEM(items.shape, f32),
            pltpu.VMEM((B * B // 2, LANES), f32), pltpu.SemaphoreType.DMA((7,)),
        ],
        compiler_params=params(16),
    )(coords, counts, values, observed, items, table)


def user_equations(places, weeks, mask, weighted, irows, table):
    return pl.pallas_call(
        user_kernel,
        out_shape=(
            pltpu.VMEM((UBD * B, WIDTH), LINK),
            pltpu.VMEM((2, B, WIDTH), bf16),
            pltpu.VMEM((2, B // SIDE, B, LANES), f32),
        ),
        in_specs=[smem()] + [vmem()] * 5,
        out_specs=[vmem()] * 3,
        scratch_shapes=[pltpu.VMEM((UBD * B, WIDTH), f32), pltpu.VMEM((UBD * B, R), f32)],
        compiler_params=params(16),
    )(places, weeks, mask, weighted, irows, table)


def item_equations(places, turned, moment, users, wpairs, table):
    return pl.pallas_call(
        item_kernel,
        out_shape=pltpu.VMEM((IBD * B, WIDTH), LINK),
        in_specs=[smem()] + [vmem()] * 5,
        out_specs=vmem(),
        scratch_shapes=[pltpu.VMEM((IBD * B, WIDTH), f32), pltpu.VMEM((IBD * B, R), f32)],
        compiler_params=params(16),
    )(places, turned, moment, users, wpairs, table)


def solve(parts, copies):
    return pl.pallas_call(
        solve_kernel,
        out_shape=(jax.ShapeDtypeStruct((T, R), f32), copies),
        in_specs=[vmem()],
        out_specs=(vmem(), vmem()),
        compiler_params=params(16),
    )(parts)


def week_kernel(weeks, out):
    rows = weeks[...]
    row = jnp.concatenate([
        jnp.concatenate([rows[k * PACK + n:k * PACK + n + 1] for n in range(PACK)], axis=1) for k in range(2)
    ], axis=0)
    out[...] = jnp.broadcast_to(row[None], out.shape).astype(bf16)


def week_copies(weeks, peers):
    return pl.pallas_call(
        week_kernel,
        out_shape=pltpu.VMEM((peers, 2, LANES), bf16),
        in_specs=[vmem()],
        out_specs=vmem(),
        compiler_params=params(16),
    )(weeks)


def copies_kernel(x, out):
    rows = x[...].reshape(out.shape[1:])
    out[...] = jnp.broadcast_to(rows[None], out.shape)


def copies_of(x, peers):
    return pl.pallas_call(
        copies_kernel,
        out_shape=pltpu.VMEM((peers, x.shape[0], LANES), x.dtype),
        in_specs=[vmem()],
        out_specs=vmem(),
        compiler_params=params(16),
    )(x)


def exchange(x, axis):
    return lax.all_to_all(x, axis, 0, 0, tiled=True)


def shards(values, observed, coords, counts, item_factors, week_factors):
    n_slab, n_fib = lax.axis_size(SLABS), lax.axis_size(FIBS)
    pair = lax.all_gather(week_factors, "core", axis=0, tiled=True)
    copies = week_copies(pair, n_slab * n_fib // 2)
    weeks = exchange(copies, ("z", "x", "y"))
    mask, turned, weighted, irows, table, places = prepare(
        coords[0], counts, values[0], observed[0], item_factors.T, jnp.asarray(TABLE, bf16)
    )
    parts, wpairs, moment = user_equations(places, weeks, mask, weighted, irows, table)
    user_out, copies = solve(exchange(parts, FIBS), pltpu.VMEM((n_fib * T, LANES), bf16))
    users = exchange(copies, FIBS)
    parts = item_equations(places, turned, moment, users, wpairs, table)
    _, copies = solve(exchange(parts, SLABS), pltpu.VMEM((n_slab, T, LANES), f32))
    item_updated = exchange(copies, SLABS).reshape(IBD * B, LANES)[:, :R]
    return (user_out, item_updated)


def solution(mesh):
    fine = jax.sharding.Mesh(mesh.devices.reshape(8, 2, 4, 8), SLABS + FIBS)
    in_specs = (
        P(SLABS, FIBS, None, None),
        P(SLABS, FIBS, None, None),
        P(SLABS, FIBS, None),
        P(SLABS, FIBS),
        P(FIBS, None),
        P(SLABS + FIBS, None),
    )
    out_specs = (P(SLABS + FIBS, None), P(FIBS, None))
    return jax.shard_map(shards, mesh=fine, in_specs=in_specs, out_specs=out_specs, check_vma=False)
```

```python
import jax
import jax.numpy as jnp
import numpy as np
from jax import lax
from jax.experimental import pallas as pl
from jax.experimental.pallas import tpu as pltpu
from jax.sharding import PartitionSpec as P

B = 64
R = 32
UBD = 4
IBD = 2
T = 8
LANES = 128
SIDE = 4
CHUNK = SIDE * B
PACK = LANES // R
WROWS = B // PACK
FIB = 32
SLABS, FIBS = ("z", "core"), ("x", "y")
ridge_weight = 1.0
precise = lax.Precision.HIGHEST
LINK = jnp.bfloat16
f32 = jnp.float32
bf16 = jnp.bfloat16


def tables():
    start, left, right = {}, [], []
    for r in range(R):
        start[r] = len(left)
        for s in range(r // T * T, R):
            left.append(r)
            right.append(s)
    width = len(left)
    one = np.zeros((R, width), np.float32)
    two = np.zeros((R, width), np.float32)
    for k, (r, s) in enumerate(zip(left, right)):
        if s >= r:
            one[r, k] = 1
            two[s, k] = 1
    put = np.zeros((LANES, width), np.float32)
    for j in range(R // T):
        row5, row6, row7 = (start[j * T + n] for n in (5, 6, 7))
        for n in range(7):
            put[j * T + n, row7 + n] = 1
        put[j * T + 7, row6] = 1
        for n in range(1, 6):
            put[R + j * T + n, row6 + n] = 1
        put[R + j * T, row5] = 1
        put[R + j * T + 6, row5 + 1] = 1
        put[R + j * T + 7, row5 + 2] = 1
    return start, width, one, two, put


START, WIDTH, ONE, TWO, PUT = tables()
TABLE = np.concatenate([ONE, TWO, PUT[:2 * R]])


def dot(a, b, dims=(1, 0), precision=None):
    return lax.dot_general(
        a, b, (((dims[0],), (dims[1],)), ((), ())), preferred_element_type=f32, precision=precision
    )


def iota(shape, dim):
    return lax.broadcasted_iota(jnp.int32, shape, dim)


def week_blocks(weeks, one, two, starts):
    packed = []
    for start in starts:
        slab, part = start // (FIB // WROWS), start % (FIB // WROWS)
        both = weeks[pl.ds(slab // 2 * FIB + part * WROWS, WROWS)].astype(f32)
        packed.append(jnp.where(slab % 2 == 0, both[:, 0], both[:, 1]))
    packed = jnp.concatenate(packed).astype(bf16)
    count = len(starts) * B
    spread = (iota((count, count // PACK), 0) // PACK == iota((count, count // PACK), 1)).astype(f32).astype(bf16)
    rows = dot(spread, packed)
    own = iota(rows.shape, 0) % PACK == iota(rows.shape, 1) // R
    rows = jnp.where(own, rows, 0.0).astype(bf16)
    pairs = dot(rows, jnp.concatenate([one] * PACK)) * dot(rows, jnp.concatenate([two] * PACK))
    return pairs.astype(bf16), dot(rows, fold())


def together(first, second, same):
    return first + jnp.where(same, second, 0.0), second + jnp.where(same, first, 0.0)


def unfold(x):
    return sum(x[:, n * R:(n + 1) * R] for n in range(PACK))


def fold():
    return (iota((LANES, LANES), 0) % R == iota((LANES, LANES), 1) % R).astype(f32).astype(bf16)


def three(x, axis):
    high = x.astype(bf16).astype(f32)
    middle = (x - high).astype(bf16).astype(f32)
    low = (x - high) - middle
    return jnp.concatenate([high, middle, low, jnp.zeros_like(low)], axis=axis).astype(bf16)


def send_form(gram, rhs, put):
    high = rhs.astype(bf16).astype(f32)
    parts = jnp.concatenate([high, rhs - high], axis=1).astype(bf16)
    return (gram + dot(parts, put)).astype(LINK)


def turn(own, strips):
    pairs = B // 2
    for t in range(pairs):
        strips[t * B:(t + 1) * B] = own[:, t * LANES:(t + 1) * LANES]
    first = iota((pairs, LANES), 1) < B
    tiles = []
    for v in range(pairs):
        a, b = (strips[pl.ds(2 * v + n, pairs, stride=B)] for n in range(2))
        even = jnp.where(first, a, pltpu.roll(b, B, 1))
        odd = jnp.where(first, pltpu.roll(a, B, 1), b)
        tiles.append(jnp.concatenate([even, odd]).astype(bf16))
    place = iota((B, B), 1)
    order = place % pairs * 2 + place // pairs == iota((B, B), 0)
    return dot(jnp.where(order, 1.0, 0.0).astype(bf16), jnp.concatenate(tiles, axis=1)).astype(bf16)


def four_a_row(rows):
    count = rows.shape[0]
    own = iota(rows.shape, 0) % PACK == iota(rows.shape, 1) // R
    parts = three(jnp.where(own, rows, 0.0), 0)
    pick = iota((count // PACK, 4 * count), 1) % count // PACK == iota((count // PACK, 4 * count), 0)
    return dot(jnp.where(pick, 1.0, 0.0).astype(bf16), parts)


def paired(mask, slot, pairs, wp):
    total = jnp.zeros((B, WIDTH), f32)
    step = 2 * SIDE
    for c in range(0, B, step):
        outer = []
        for i in range(c, c + step):
            row = jnp.broadcast_to(pairs[i:i + 1], (16, WIDTH)).astype(bf16)
            outer.append((wp * row[None]).reshape(B, WIDTH))
        total += dot(mask[slot, :, c * B:(c + step) * B].astype(bf16), jnp.concatenate(outer))
    return total


def prepare_kernel(coords_in, counts, values_in, observed_in, items_in, table_in, mask, turned, weighted, irows,
                   table, places, coords, values, observed, items, strips, sems):
    moves = []
    for n, (source, target) in enumerate((
        (table_in, table.at[:TABLE.shape[0]]), (items_in, items), (observed_in.at[0], observed.at[0]), (values_in.at[0], values.at[0]),
        (observed_in.at[1], observed.at[1]), (values_in.at[1], values.at[1]), (coords_in, coords),
    )):
        moves.append(pltpu.make_async_copy(source, target, sems.at[n]))
        moves[n].start()
    moves[0].wait()
    moves[1].wait()
    rows = three(items[...], 0)
    pairs = dot(rows, jnp.concatenate([table[:R]] * PACK), (0, 0))
    pairs *= dot(rows, jnp.concatenate([table[R:2 * R]] * PACK), (0, 0))
    table[TABLE.shape[0]:] = pairs.astype(bf16)
    irows[...] = four_a_row(dot(rows, fold(), (0, 0)))
    for slot in range(2):
        moves[2 + 2 * slot].wait()
        moves[3 + 2 * slot].wait()
        own = observed[slot].astype(f32)
        if slot > 0:
            own = jnp.where(counts[0, 0] > slot, own, 0.0)
        mask[slot] = own.astype(bf16).astype(jnp.float8_e4m3fn)
        weighted[slot] = (values[slot].astype(f32) * own).astype(bf16)
        turned[slot] = turn(own, strips).astype(turned.dtype)
    moves[6].wait()
    for slot in range(2):
        for n in range(3):
            places[slot, n] = coords[slot, n]


def user_kernel(places, weeks, mask, weighted, irows, table, out, wpairs, moment):
    one, two, put = table[:R], table[R:2 * R], table[2 * R:TABLE.shape[0]]
    pairs, rows = week_blocks(weeks, one, two, [places[slot, 2] for slot in range(2)])
    out[...] = jnp.zeros_like(out)
    apart = iota((CHUNK, LANES), 0) // B == iota((CHUNK, LANES), 1) // R
    gram, rhs = [], []
    for slot in range(2):
        ibase = pl.multiple_of(places[slot, 1] * B, B)
        wp, wr = pairs[slot * B:(slot + 1) * B], rows[slot * B:(slot + 1) * B]
        wpairs[slot] = wp
        ip = table[pl.ds(pl.multiple_of(TABLE.shape[0] + ibase, B), B), :].astype(f32)
        ir = irows[pl.ds(pl.multiple_of(places[slot, 1] * (B // PACK), B // PACK), B // PACK), :]
        every = jnp.concatenate([weighted[slot, :, c * CHUNK:(c + 1) * CHUNK] for c in range(B // SIDE)])
        every = dot(every, jnp.where(apart, jnp.concatenate([wr] * SIDE), 0.0).astype(bf16))
        total = jnp.zeros((B, LANES), f32)
        for c in range(B // SIDE):
            here = every[c * B:(c + 1) * B]
            moment[slot, c] = here
            total += here * ir[c:c + 1]
        rhs.append(total)
        gram.append(paired(mask, slot, ip, wp.reshape(B // 16, 16, WIDTH)))
    same = places[0, 0] == places[1, 0]
    rhs = unfold(jnp.concatenate(together(*rhs, same)))
    sent = send_form(jnp.concatenate(together(*gram, same)), rhs, put)
    for slot in range(2):
        out[pl.ds(pl.multiple_of(places[slot, 0] * B, B), B), :] = sent[slot * B:(slot + 1) * B]


def item_kernel(places, turned, moment, users, wpairs, table, out):
    one, two, put = table[:R], table[R:2 * R], table[2 * R:TABLE.shape[0]]
    rows = jnp.concatenate([users[pl.ds(pl.multiple_of(places[slot, 0] * B, B), B), :] for slot in range(2)])
    pairs = dot(rows, jnp.concatenate([one] * PACK)) * dot(rows, jnp.concatenate([two] * PACK))
    rows = dot(rows, fold())
    out[...] = jnp.zeros_like(out)
    gram, sums = [], []
    for slot in range(2):
        here = slice(slot * B, (slot + 1) * B)
        gram.append(paired(turned, slot, pairs[here], wpairs[slot].reshape(B // 16, 16, WIDTH)))
        sums.append(jnp.sum(moment[slot] * rows[here][None], axis=1))
    parts = three(jnp.concatenate(sums), 0)
    count = 2 * B
    spread = iota((count, count), 1) % (count // PACK) == iota((count, count), 0) // PACK
    rhs = dot(jnp.where(spread, 1.0, 0.0).astype(bf16), parts)
    rhs = jnp.where(iota(rhs.shape, 0) % PACK == iota(rhs.shape, 1) // R, rhs, 0.0)
    same = places[0, 1] == places[1, 1]
    rhs = jnp.concatenate(together(rhs[:B], rhs[B:], same))
    high = rhs.astype(bf16).astype(f32)
    parts = jnp.concatenate([high, rhs - high], axis=1).astype(bf16)
    wide = jnp.concatenate([put[:R]] * PACK + [put[R:]] * PACK)
    sent = (jnp.concatenate(together(*gram, same)) + dot(parts, wide)).astype(LINK)
    for slot in range(2):
        out[pl.ds(pl.multiple_of(places[slot, 1] * B, B), B), :] = sent[slot * B:(slot + 1) * B]


def solve_kernel(parts, out, copies):
    count = parts.shape[0]
    pick = (iota((count, LANES), 0) % T == iota((count, LANES), 1)).astype(f32)
    if LINK == bf16:
        packed = dot(parts[...], pick.astype(bf16), (0, 0))
    else:
        packed = dot(parts[...], pick, (0, 0), precise)
    sub = iota((T, LANES), 0)

    def tile(r, t):
        first = START[r] + (t - r // T) * T
        return packed[first:first + T]

    def spread(x, n):
        return jnp.broadcast_to(x[n:n + 1], (T, LANES))

    tiles = R // T
    rows = {}
    for r in range(R):
        for t in range(r // T, tiles):
            x = tile(r, t)
            rows[r, t] = x + jnp.where(sub == r % T, ridge_weight, 0.0) if t == r // T else x
    side = []
    for j in range(tiles):
        row5, row6, row7 = (tile(j * T + n, j) for n in (5, 6, 7))
        high = jnp.where(sub == 7, spread(row6, 0), row7)
        low = jnp.where(sub == 0, row5, row6)
        low = jnp.where(sub == 6, spread(row5, 1), low)
        low = jnp.where(sub == 7, spread(row5, 2), low)
        side.append(high + low)
    factor, right = {}, []
    for k in range(R):
        own = k // T
        inverse = 1.0 / spread(rows[k, own], k % T)
        scaled = {t: rows[k, t] * inverse for t in range(own, tiles)}
        mine = spread(side[own], k % T)
        right.append(mine * inverse)
        for t in range(own, tiles):
            side[t] = side[t] - scaled[t] * mine
        for r in range(k + 1, R):
            factor[k, r] = spread(scaled[r // T], r % T)
            for t in range(r // T, tiles):
                rows[r, t] = rows[r, t] - factor[k, r] * rows[k, t]
    answer = []
    for s in range(R - 1, -1, -1):
        for k in range(s):
            right[k] = right[k] - factor[k, s] * right[s]
    for j in range(tiles):
        x = right[j * T]
        for n in range(1, T):
            x = jnp.where(sub == n, right[j * T + n], x)
        answer.append(x)
    answer = jnp.concatenate(answer + [jnp.zeros((LANES - R, LANES), f32)], axis=0)
    answer = jnp.transpose(answer)[:T]
    out[...] = answer[:, :R]
    if copies.dtype == bf16:
        answer = three(answer[:, :R], 1).astype(f32)
        copies[...] = jnp.concatenate([answer] * (copies.shape[0] // T)).astype(bf16)
    else:
        copies[...] = jnp.broadcast_to(answer[None], copies.shape)


def vmem():
    return pl.BlockSpec(memory_space=pltpu.VMEM)


def smem():
    return pl.BlockSpec(memory_space=pltpu.SMEM)


def anywhere():
    return pl.BlockSpec(memory_space=pl.ANY)


def params(mib):
    return pltpu.CompilerParams(vmem_limit_bytes=mib * 1024 * 1024)


def prepare(coords, counts, values, observed, items, table):
    coords, values, observed, items, table = (
        pltpu.with_memory_space_constraint(x, pltpu.HBM) for x in (coords, values, observed, items, table)
    )
    return pl.pallas_call(
        prepare_kernel,
        out_shape=(
            pltpu.VMEM(values.shape, jnp.float8_e4m3fn),
            pltpu.VMEM(values.shape, jnp.float8_e4m3fn),
            pltpu.VMEM(values.shape, bf16),
            pltpu.VMEM((IBD * B // PACK, LANES), f32),
            pltpu.VMEM((table.shape[0] + IBD * B, WIDTH), bf16),
            jax.ShapeDtypeStruct((2, 3), jnp.int32),
        ),
        in_specs=[anywhere(), smem()] + [anywhere()] * 4,
        out_specs=[vmem()] * 5 + [smem()],
        scratch_shapes=[
            pltpu.SMEM(coords.shape, jnp.int32), pltpu.VMEM(values.shape, bf16), pltpu.VMEM(observed.shape, jnp.int32), pltpu.VMEM(items.shape, f32),
            pltpu.VMEM((B * B // 2, LANES), f32), pltpu.SemaphoreType.DMA((7,)),
        ],
        compiler_params=params(16),
    )(coords, counts, values, observed, items, table)


def user_equations(places, weeks, mask, weighted, irows, table):
    return pl.pallas_call(
        user_kernel,
        out_shape=(
            pltpu.VMEM((UBD * B, WIDTH), LINK),
            pltpu.VMEM((2, B, WIDTH), bf16),
            pltpu.VMEM((2, B // SIDE, B, LANES), f32),
        ),
        in_specs=[smem()] + [vmem()] * 5,
        out_specs=[vmem()] * 3,
        compiler_params=params(16),
    )(places, weeks, mask, weighted, irows, table)


def item_equations(places, turned, moment, users, wpairs, table):
    return pl.pallas_call(
        item_kernel,
        out_shape=pltpu.VMEM((IBD * B, WIDTH), LINK),
        in_specs=[smem()] + [vmem()] * 5,
        out_specs=vmem(),
        compiler_params=params(16),
    )(places, turned, moment, users, wpairs, table)


def solve(parts, copies):
    return pl.pallas_call(
        solve_kernel,
        out_shape=(jax.ShapeDtypeStruct((T, R), f32), copies),
        in_specs=[vmem()],
        out_specs=(vmem(), vmem()),
        compiler_params=params(16),
    )(parts)


def week_kernel(weeks, out):
    rows = weeks[...]
    row = jnp.concatenate([
        jnp.concatenate([rows[k * PACK + n:k * PACK + n + 1] for n in range(PACK)], axis=1) for k in range(2)
    ], axis=0)
    out[...] = jnp.broadcast_to(row[None], out.shape).astype(bf16)


def week_copies(weeks, peers):
    return pl.pallas_call(
        week_kernel,
        out_shape=pltpu.VMEM((peers, 2, LANES), bf16),
        in_specs=[vmem()],
        out_specs=vmem(),
        compiler_params=params(16),
    )(weeks)


def copies_kernel(x, out):
    rows = x[...].reshape(out.shape[1:])
    out[...] = jnp.broadcast_to(rows[None], out.shape)


def copies_of(x, peers):
    return pl.pallas_call(
        copies_kernel,
        out_shape=pltpu.VMEM((peers, x.shape[0], LANES), x.dtype),
        in_specs=[vmem()],
        out_specs=vmem(),
        compiler_params=params(16),
    )(x)


def exchange(x, axis):
    return lax.all_to_all(x, axis, 0, 0, tiled=True)


def shards(values, observed, coords, counts, item_factors, week_factors):
    n_slab, n_fib = lax.axis_size(SLABS), lax.axis_size(FIBS)
    pair = lax.all_gather(week_factors, "core", axis=0, tiled=True)
    copies = week_copies(pair, n_slab * n_fib // 2)
    weeks = exchange(copies, ("z", "x", "y"))
    mask, turned, weighted, irows, table, places = prepare(
        coords[0], counts, values[0], observed[0], item_factors.T, jnp.asarray(TABLE, bf16)
    )
    parts, wpairs, moment = user_equations(places, weeks, mask, weighted, irows, table)
    user_out, copies = solve(exchange(parts, FIBS), pltpu.VMEM((n_fib * T, LANES), bf16))
    users = exchange(copies, FIBS)
    parts = item_equations(places, turned, moment, users, wpairs, table)
    _, copies = solve(exchange(parts, SLABS), pltpu.VMEM((n_slab, T, LANES), f32))
    item_updated = exchange(copies, SLABS).reshape(IBD * B, LANES)[:, :R]
    return (user_out, item_updated)


def solution(mesh):
    fine = jax.sharding.Mesh(mesh.devices.reshape(8, 2, 4, 8), SLABS + FIBS)
    in_specs = (
        P(SLABS, FIBS, None, None),
        P(SLABS, FIBS, None, None),
        P(SLABS, FIBS, None),
        P(SLABS, FIBS),
        P(FIBS, None),
        P(SLABS + FIBS, None),
    )
    out_specs = (P(SLABS + FIBS, None), P(FIBS, None))
    return jax.shard_map(shards, mesh=fine, in_specs=in_specs, out_specs=out_specs, check_vma=False)
```

```python
import jax
import jax.numpy as jnp
import numpy as np
from jax import lax
from jax.experimental import pallas as pl
from jax.experimental.pallas import tpu as pltpu
from jax.sharding import PartitionSpec as P

B = 64
R = 32
UBD = 4
IBD = 2
T = 8
LANES = 128
SIDE = 4
CHUNK = SIDE * B
PACK = LANES // R
WROWS = B // PACK
FIB = 32
SLABS, FIBS = ("z", "core"), ("x", "y")
ridge_weight = 1.0
precise = lax.Precision.HIGHEST
LINK = jnp.bfloat16
f32 = jnp.float32
bf16 = jnp.bfloat16


def tables():
    start, left, right = {}, [], []
    for r in range(R):
        start[r] = len(left)
        for s in range(r // T * T, R):
            left.append(r)
            right.append(s)
    width = len(left)
    one = np.zeros((R, width), np.float32)
    two = np.zeros((R, width), np.float32)
    for k, (r, s) in enumerate(zip(left, right)):
        if s >= r:
            one[r, k] = 1
            two[s, k] = 1
    put = np.zeros((LANES, width), np.float32)
    for j in range(R // T):
        row5, row6, row7 = (start[j * T + n] for n in (5, 6, 7))
        for n in range(7):
            put[j * T + n, row7 + n] = 1
        put[j * T + 7, row6] = 1
        for n in range(1, 6):
            put[R + j * T + n, row6 + n] = 1
        put[R + j * T, row5] = 1
        put[R + j * T + 6, row5 + 1] = 1
        put[R + j * T + 7, row5 + 2] = 1
    return start, width, one, two, put


START, WIDTH, ONE, TWO, PUT = tables()
TABLE = np.concatenate([ONE, TWO, PUT[:2 * R]])


def dot(a, b, dims=(1, 0), precision=None):
    return lax.dot_general(
        a, b, (((dims[0],), (dims[1],)), ((), ())), preferred_element_type=f32, precision=precision
    )


def iota(shape, dim):
    return lax.broadcasted_iota(jnp.int32, shape, dim)


def week_blocks(weeks, one, two, starts):
    packed = []
    for start in starts:
        slab, part = start // (FIB // WROWS), start % (FIB // WROWS)
        both = weeks[pl.ds(slab // 2 * FIB + part * WROWS, WROWS)].astype(f32)
        packed.append(jnp.where(slab % 2 == 0, both[:, 0], both[:, 1]))
    packed = jnp.concatenate(packed).astype(bf16)
    count = len(starts) * B
    spread = (iota((count, count // PACK), 0) // PACK == iota((count, count // PACK), 1)).astype(f32).astype(bf16)
    rows = dot(spread, packed)
    own = iota(rows.shape, 0) % PACK == iota(rows.shape, 1) // R
    rows = jnp.where(own, rows, 0.0).astype(bf16)
    pairs = dot(rows, jnp.concatenate([one] * PACK)) * dot(rows, jnp.concatenate([two] * PACK))
    return pairs.astype(bf16), dot(rows, fold())


def together(first, second, same):
    return first + jnp.where(same, second, 0.0), second + jnp.where(same, first, 0.0)


def unfold(x):
    return sum(x[:, n * R:(n + 1) * R] for n in range(PACK))


def fold():
    return (iota((LANES, LANES), 0) % R == iota((LANES, LANES), 1) % R).astype(f32).astype(bf16)


def three(x, axis):
    high = x.astype(bf16).astype(f32)
    middle = (x - high).astype(bf16).astype(f32)
    low = (x - high) - middle
    return jnp.concatenate([high, middle, low, jnp.zeros_like(low)], axis=axis).astype(bf16)


def send_form(gram, rhs, put):
    high = rhs.astype(bf16).astype(f32)
    parts = jnp.concatenate([high, rhs - high], axis=1).astype(bf16)
    return (gram + dot(parts, put)).astype(LINK)


def turn(own, strips):
    pairs = B // 2
    for t in range(pairs):
        strips[t * B:(t + 1) * B] = own[:, t * LANES:(t + 1) * LANES]
    first = iota((pairs, LANES), 1) < B
    tiles = []
    for v in range(pairs):
        a, b = (strips[pl.ds(2 * v + n, pairs, stride=B)] for n in range(2))
        even = jnp.where(first, a, pltpu.roll(b, B, 1))
        odd = jnp.where(first, pltpu.roll(a, B, 1), b)
        tiles.append(jnp.concatenate([even, odd]).astype(bf16))
    place = iota((B, B), 1)
    order = place % pairs * 2 + place // pairs == iota((B, B), 0)
    return dot(jnp.where(order, 1.0, 0.0).astype(bf16), jnp.concatenate(tiles, axis=1)).astype(bf16)


def four_a_row(rows):
    count = rows.shape[0]
    own = iota(rows.shape, 0) % PACK == iota(rows.shape, 1) // R
    parts = three(jnp.where(own, rows, 0.0), 0)
    pick = iota((count // PACK, 4 * count), 1) % count // PACK == iota((count // PACK, 4 * count), 0)
    return dot(jnp.where(pick, 1.0, 0.0).astype(bf16), parts)


def paired(mask, slot, pairs, wp):
    total = jnp.zeros((B, WIDTH), f32)
    step = 2 * SIDE
    for c in range(0, B, step):
        outer = []
        for i in range(c, c + step):
            row = jnp.broadcast_to(pairs[i:i + 1], (16, WIDTH)).astype(bf16)
            outer.append((wp * row[None]).reshape(B, WIDTH))
        total += dot(mask[slot, :, c * B:(c + step) * B].astype(bf16), jnp.concatenate(outer))
    return total


def prepare_kernel(coords_in, counts, values_in, observed_in, items_in, table_in, mask, turned, weighted, irows,
                   table, places, coords, values, observed, items, strips, sems):
    moves = []
    for n, (source, target) in enumerate((
        (table_in, table.at[:TABLE.shape[0]]), (items_in, items), (observed_in.at[0], observed.at[0]), (values_in.at[0], values.at[0]),
        (observed_in.at[1], observed.at[1]), (values_in.at[1], values.at[1]), (coords_in, coords),
    )):
        moves.append(pltpu.make_async_copy(source, target, sems.at[n]))
        moves[n].start()
    moves[0].wait()
    moves[1].wait()
    rows = three(items[...], 0)
    pairs = dot(rows, jnp.concatenate([table[:R]] * PACK), (0, 0))
    pairs *= dot(rows, jnp.concatenate([table[R:2 * R]] * PACK), (0, 0))
    table[TABLE.shape[0]:] = pairs.astype(bf16)
    irows[...] = four_a_row(dot(rows, fold(), (0, 0)))
    for slot in range(2):
        moves[2 + 2 * slot].wait()
        moves[3 + 2 * slot].wait()
        own = observed[slot].astype(f32)
        if slot > 0:
            own = jnp.where(counts[0, 0] > slot, own, 0.0)
        mask[slot] = own.astype(bf16).astype(jnp.float8_e4m3fn)
        weighted[slot] = (values[slot].astype(f32) * own).astype(bf16)
        turned[slot] = turn(own, strips).astype(turned.dtype)
    moves[6].wait()
    for slot in range(2):
        for n in range(3):
            places[slot, n] = coords[slot, n]


def user_kernel(places, weeks, mask, weighted, irows, table, out, wpairs, moment):
    one, two, put = table[:R], table[R:2 * R], table[2 * R:TABLE.shape[0]]
    pairs, rows = week_blocks(weeks, one, two, [places[slot, 2] for slot in range(2)])
    out[...] = jnp.zeros_like(out)
    apart = iota((CHUNK, LANES), 0) // B == iota((CHUNK, LANES), 1) // R
    gram, rhs = [], []
    for slot in range(2):
        ibase = pl.multiple_of(places[slot, 1] * B, B)
        wp, wr = pairs[slot * B:(slot + 1) * B], rows[slot * B:(slot + 1) * B]
        wpairs[slot] = wp
        ip = table[pl.ds(pl.multiple_of(TABLE.shape[0] + ibase, B), B), :].astype(f32)
        ir = irows[pl.ds(pl.multiple_of(places[slot, 1] * (B // PACK), B // PACK), B // PACK), :]
        every = jnp.concatenate([weighted[slot, :, c * CHUNK:(c + 1) * CHUNK] for c in range(B // SIDE)])
        every = dot(every, jnp.where(apart, jnp.concatenate([wr] * SIDE), 0.0).astype(bf16))
        total = jnp.zeros((B, LANES), f32)
        for c in range(B // SIDE):
            here = every[c * B:(c + 1) * B]
            moment[slot, c] = here
            total += here * ir[c:c + 1]
        rhs.append(total)
        gram.append(paired(mask, slot, ip, wp.reshape(B // 16, 16, WIDTH)))
    same = places[0, 0] == places[1, 0]
    rhs = unfold(jnp.concatenate(together(*rhs, same)))
    sent = send_form(jnp.concatenate(together(*gram, same)), rhs, put)
    for slot in range(2):
        out[pl.ds(pl.multiple_of(places[slot, 0] * B, B), B), :] = sent[slot * B:(slot + 1) * B]


def item_kernel(places, turned, moment, users, wpairs, table, out):
    one, two, put = table[:R], table[R:2 * R], table[2 * R:TABLE.shape[0]]
    rows = jnp.concatenate([users[pl.ds(pl.multiple_of(places[slot, 0] * B, B), B), :] for slot in range(2)])
    pairs = dot(rows, jnp.concatenate([one] * PACK)) * dot(rows, jnp.concatenate([two] * PACK))
    rows = dot(rows, fold())
    out[...] = jnp.zeros_like(out)
    gram, sums = [], []
    for slot in range(2):
        here = slice(slot * B, (slot + 1) * B)
        gram.append(paired(turned, slot, pairs[here], wpairs[slot].reshape(B // 16, 16, WIDTH)))
        sums.append(jnp.sum(moment[slot] * rows[here][None], axis=1))
    parts = three(jnp.concatenate(sums), 0)
    count = 2 * B
    spread = iota((count, count), 1) % (count // PACK) == iota((count, count), 0) // PACK
    rhs = dot(jnp.where(spread, 1.0, 0.0).astype(bf16), parts)
    rhs = jnp.where(iota(rhs.shape, 0) % PACK == iota(rhs.shape, 1) // R, rhs, 0.0)
    same = places[0, 1] == places[1, 1]
    rhs = jnp.concatenate(together(rhs[:B], rhs[B:], same))
    high = rhs.astype(bf16).astype(f32)
    parts = jnp.concatenate([high, rhs - high], axis=1).astype(bf16)
    wide = jnp.concatenate([put[:R]] * PACK + [put[R:]] * PACK)
    sent = (jnp.concatenate(together(*gram, same)) + dot(parts, wide)).astype(LINK)
    for slot in range(2):
        out[pl.ds(pl.multiple_of(places[slot, 1] * B, B), B), :] = sent[slot * B:(slot + 1) * B]


def solve_kernel(parts, out, copies):
    count = parts.shape[0]
    pick = (iota((count, LANES), 0) % T == iota((count, LANES), 1)).astype(f32)
    if LINK == bf16:
        packed = dot(parts[...], pick.astype(bf16), (0, 0))
    else:
        packed = dot(parts[...], pick, (0, 0), precise)
    sub = iota((T, LANES), 0)

    def tile(r, t):
        first = START[r] + (t - r // T) * T
        return packed[first:first + T]

    def spread(x, n):
        return jnp.broadcast_to(x[n:n + 1], (T, LANES))

    tiles = R // T
    rows = {}
    for r in range(R):
        for t in range(r // T, tiles):
            x = tile(r, t)
            rows[r, t] = x + jnp.where(sub == r % T, ridge_weight, 0.0) if t == r // T else x
    side = []
    for j in range(tiles):
        row5, row6, row7 = (tile(j * T + n, j) for n in (5, 6, 7))
        high = jnp.where(sub == 7, spread(row6, 0), row7)
        low = jnp.where(sub == 0, row5, row6)
        low = jnp.where(sub == 6, spread(row5, 1), low)
        low = jnp.where(sub == 7, spread(row5, 2), low)
        side.append(high + low)
    factor, right = {}, []
    for k in range(R):
        own = k // T
        inverse = 1.0 / spread(rows[k, own], k % T)
        scaled = {t: rows[k, t] * inverse for t in range(own, tiles)}
        mine = spread(side[own], k % T)
        right.append(mine * inverse)
        for t in range(own, tiles):
            side[t] = side[t] - scaled[t] * mine
        for r in range(k + 1, R):
            factor[k, r] = spread(scaled[r // T], r % T)
            for t in range(r // T, tiles):
                rows[r, t] = rows[r, t] - factor[k, r] * rows[k, t]
    answer = []
    for s in range(R - 1, -1, -1):
        for k in range(s):
            right[k] = right[k] - factor[k, s] * right[s]
    for j in range(tiles):
        x = right[j * T]
        for n in range(1, T):
            x = jnp.where(sub == n, right[j * T + n], x)
        answer.append(x)
    answer = jnp.concatenate(answer + [jnp.zeros((LANES - R, LANES), f32)], axis=0)
    answer = jnp.transpose(answer)[:T]
    out[...] = answer[:, :R]
    if copies.dtype == bf16:
        answer = three(answer[:, :R], 1).astype(f32)
        copies[...] = jnp.concatenate([answer] * (copies.shape[0] // T)).astype(bf16)
    else:
        copies[...] = jnp.broadcast_to(answer[None], copies.shape)


def vmem():
    return pl.BlockSpec(memory_space=pltpu.VMEM)


def smem():
    return pl.BlockSpec(memory_space=pltpu.SMEM)


def anywhere():
    return pl.BlockSpec(memory_space=pl.ANY)


def params(mib):
    return pltpu.CompilerParams(vmem_limit_bytes=mib * 1024 * 1024)


def prepare(coords, counts, values, observed, items, table):
    coords, values, observed, items, table = (
        pltpu.with_memory_space_constraint(x, pltpu.HBM) for x in (coords, values, observed, items, table)
    )
    return pl.pallas_call(
        prepare_kernel,
        out_shape=(
            pltpu.VMEM(values.shape, jnp.float8_e4m3fn),
            pltpu.VMEM(values.shape, jnp.float8_e4m3fn),
            pltpu.VMEM(values.shape, bf16),
            pltpu.VMEM((IBD * B // PACK, LANES), f32),
            pltpu.VMEM((table.shape[0] + IBD * B, WIDTH), bf16),
            jax.ShapeDtypeStruct((2, 3), jnp.int32),
        ),
        in_specs=[anywhere(), smem()] + [anywhere()] * 4,
        out_specs=[vmem()] * 5 + [smem()],
        scratch_shapes=[
            pltpu.SMEM(coords.shape, jnp.int32), pltpu.VMEM(values.shape, bf16), pltpu.VMEM(observed.shape, jnp.int32), pltpu.VMEM(items.shape, f32),
            pltpu.VMEM((B * B // 2 + B, LANES), f32), pltpu.SemaphoreType.DMA((7,)),
        ],
        compiler_params=params(16),
    )(coords, counts, values, observed, items, table)


def user_equations(places, weeks, mask, weighted, irows, table):
    return pl.pallas_call(
        user_kernel,
        out_shape=(
            pltpu.VMEM((UBD * B, WIDTH), LINK),
            pltpu.VMEM((2, B, WIDTH), bf16),
            pltpu.VMEM((2, B // SIDE, B, LANES), f32),
        ),
        in_specs=[smem()] + [vmem()] * 5,
        out_specs=[vmem()] * 3,
        compiler_params=params(16),
    )(places, weeks, mask, weighted, irows, table)


def item_equations(places, turned, moment, users, wpairs, table):
    return pl.pallas_call(
        item_kernel,
        out_shape=pltpu.VMEM((IBD * B, WIDTH), LINK),
        in_specs=[smem()] + [vmem()] * 5,
        out_specs=vmem(),
        compiler_params=params(16),
    )(places, turned, moment, users, wpairs, table)


def solve(parts, copies):
    return pl.pallas_call(
        solve_kernel,
        out_shape=(jax.ShapeDtypeStruct((T, R), f32), copies),
        in_specs=[vmem()],
        out_specs=(vmem(), vmem()),
        compiler_params=params(16),
    )(parts)


def week_kernel(weeks, out):
    rows = weeks[...]
    row = jnp.concatenate([
        jnp.concatenate([rows[k * PACK + n:k * PACK + n + 1] for n in range(PACK)], axis=1) for k in range(2)
    ], axis=0)
    out[...] = jnp.broadcast_to(row[None], out.shape).astype(bf16)


def week_copies(weeks, peers):
    return pl.pallas_call(
        week_kernel,
        out_shape=pltpu.VMEM((peers, 2, LANES), bf16),
        in_specs=[vmem()],
        out_specs=vmem(),
        compiler_params=params(16),
    )(weeks)


def copies_kernel(x, out):
    rows = x[...].reshape(out.shape[1:])
    out[...] = jnp.broadcast_to(rows[None], out.shape)


def copies_of(x, peers):
    return pl.pallas_call(
        copies_kernel,
        out_shape=pltpu.VMEM((peers, x.shape[0], LANES), x.dtype),
        in_specs=[vmem()],
        out_specs=vmem(),
        compiler_params=params(16),
    )(x)


def exchange(x, axis):
    return lax.all_to_all(x, axis, 0, 0, tiled=True)


def shards(values, observed, coords, counts, item_factors, week_factors):
    n_slab, n_fib = lax.axis_size(SLABS), lax.axis_size(FIBS)
    pair = lax.all_gather(week_factors, "core", axis=0, tiled=True)
    copies = week_copies(pair, n_slab * n_fib // 2)
    weeks = exchange(copies, ("z", "x", "y"))
    mask, turned, weighted, irows, table, places = prepare(
        coords[0], counts, values[0], observed[0], item_factors.T, jnp.asarray(TABLE, bf16)
    )
    parts, wpairs, moment = user_equations(places, weeks, mask, weighted, irows, table)
    user_out, copies = solve(exchange(parts, FIBS), pltpu.VMEM((n_fib * T, LANES), bf16))
    users = exchange(copies, FIBS)
    parts = item_equations(places, turned, moment, users, wpairs, table)
    _, copies = solve(exchange(parts, SLABS), pltpu.VMEM((n_slab, T, LANES), f32))
    item_updated = exchange(copies, SLABS).reshape(IBD * B, LANES)[:, :R]
    return (user_out, item_updated)


def solution(mesh):
    fine = jax.sharding.Mesh(mesh.devices.reshape(8, 2, 4, 8), SLABS + FIBS)
    in_specs = (
        P(SLABS, FIBS, None, None),
        P(SLABS, FIBS, None, None),
        P(SLABS, FIBS, None),
        P(SLABS, FIBS),
        P(FIBS, None),
        P(SLABS + FIBS, None),
    )
    out_specs = (P(SLABS + FIBS, None), P(FIBS, None))
    return jax.shard_map(shards, mesh=fine, in_specs=in_specs, out_specs=out_specs, check_vma=False)
```

```python
import jax
import jax.numpy as jnp
import numpy as np
from jax import lax
from jax.experimental import pallas as pl
from jax.experimental.pallas import tpu as pltpu
from jax.sharding import PartitionSpec as P

B = 64
R = 32
UBD = 4
IBD = 2
T = 8
LANES = 128
SIDE = 4
CHUNK = SIDE * B
PACK = LANES // R
WROWS = B // PACK
FIB = 32
SLABS, FIBS = ("z", "core"), ("x", "y")
ridge_weight = 1.0
precise = lax.Precision.HIGHEST
LINK = jnp.bfloat16
f32 = jnp.float32
bf16 = jnp.bfloat16


def tables():
    start, left, right = {}, [], []
    for r in range(R):
        start[r] = len(left)
        for s in range(r // T * T, R):
            left.append(r)
            right.append(s)
    width = len(left)
    one = np.zeros((R, width), np.float32)
    two = np.zeros((R, width), np.float32)
    for k, (r, s) in enumerate(zip(left, right)):
        if s >= r:
            one[r, k] = 1
            two[s, k] = 1
    put = np.zeros((LANES, width), np.float32)
    for j in range(R // T):
        row5, row6, row7 = (start[j * T + n] for n in (5, 6, 7))
        for n in range(7):
            put[j * T + n, row7 + n] = 1
        put[j * T + 7, row6] = 1
        for n in range(1, 6):
            put[R + j * T + n, row6 + n] = 1
        put[R + j * T, row5] = 1
        put[R + j * T + 6, row5 + 1] = 1
        put[R + j * T + 7, row5 + 2] = 1
    return start, width, one, two, put


START, WIDTH, ONE, TWO, PUT = tables()
TABLE = np.concatenate([ONE, TWO, PUT[:2 * R]])


def dot(a, b, dims=(1, 0), precision=None):
    return lax.dot_general(
        a, b, (((dims[0],), (dims[1],)), ((), ())), preferred_element_type=f32, precision=precision
    )


def iota(shape, dim):
    return lax.broadcasted_iota(jnp.int32, shape, dim)


def week_blocks(weeks, one, two, starts):
    packed = []
    for start in starts:
        slab, part = start // (FIB // WROWS), start % (FIB // WROWS)
        both = weeks[pl.ds(slab // 2 * FIB + part * WROWS, WROWS)].astype(f32)
        packed.append(jnp.where(slab % 2 == 0, both[:, 0], both[:, 1]))
    packed = jnp.concatenate(packed).astype(bf16)
    count = len(starts) * B
    spread = (iota((count, count // PACK), 0) // PACK == iota((count, count // PACK), 1)).astype(f32).astype(bf16)
    rows = dot(spread, packed)
    own = iota(rows.shape, 0) % PACK == iota(rows.shape, 1) // R
    rows = jnp.where(own, rows, 0.0).astype(bf16)
    pairs = dot(rows, jnp.concatenate([one] * PACK)) * dot(rows, jnp.concatenate([two] * PACK))
    return pairs.astype(bf16), dot(rows, fold())


def together(first, second, same):
    return first + jnp.where(same, second, 0.0), second + jnp.where(same, first, 0.0)


def unfold(x):
    return sum(x[:, n * R:(n + 1) * R] for n in range(PACK))


def fold():
    return (iota((LANES, LANES), 0) % R == iota((LANES, LANES), 1) % R).astype(f32).astype(bf16)


def three(x, axis):
    high = x.astype(bf16).astype(f32)
    middle = (x - high).astype(bf16).astype(f32)
    low = (x - high) - middle
    return jnp.concatenate([high, middle, low, jnp.zeros_like(low)], axis=axis).astype(bf16)


def send_form(gram, rhs, put):
    high = rhs.astype(bf16).astype(f32)
    parts = jnp.concatenate([high, rhs - high], axis=1).astype(bf16)
    return (gram + dot(parts, put)).astype(LINK)


def turn(own, strips):
    pairs = B // 2
    for t in range(pairs):
        strips[t * B:(t + 1) * B] = own[:, t * LANES:(t + 1) * LANES]
    first = iota((pairs, LANES), 1) < B
    tiles = []
    for v in range(pairs):
        a, b = (strips[pl.ds(2 * v + n, pairs, stride=B)] for n in range(2))
        even = jnp.where(first, a, pltpu.roll(b, B, 1))
        odd = jnp.where(first, pltpu.roll(a, B, 1), b)
        tiles.append(jnp.concatenate([even, odd]).astype(bf16))
    place = iota((B, B), 1)
    order = place % pairs * 2 + place // pairs == iota((B, B), 0)
    return dot(jnp.where(order, 1.0, 0.0).astype(bf16), jnp.concatenate(tiles, axis=1)).astype(bf16)


def four_a_row(rows):
    count = rows.shape[0]
    own = iota(rows.shape, 0) % PACK == iota(rows.shape, 1) // R
    parts = three(jnp.where(own, rows, 0.0), 0)
    pick = iota((count // PACK, 4 * count), 1) % count // PACK == iota((count // PACK, 4 * count), 0)
    return dot(jnp.where(pick, 1.0, 0.0).astype(bf16), parts)


def paired(mask, slot, pairs, wp):
    total = jnp.zeros((B, WIDTH), f32)
    step = 2 * SIDE
    for c in range(0, B, step):
        outer = []
        for i in range(c, c + step):
            row = jnp.broadcast_to(pairs[i:i + 1], (16, WIDTH)).astype(bf16)
            outer.append((wp * row[None]).reshape(B, WIDTH))
        total += dot(mask[slot, :, c * B:(c + step) * B].astype(bf16), jnp.concatenate(outer))
    return total


def prepare_kernel(coords_in, counts, values_in, observed_in, items_in, table_in, mask, turned, weighted, irows,
                   table, places, coords, values, observed, items, strips, sems):
    moves = []
    for n, (source, target) in enumerate((
        (table_in, table.at[:TABLE.shape[0]]), (items_in, items), (observed_in.at[0], observed.at[0]), (values_in.at[0], values.at[0]),
        (observed_in.at[1], observed.at[1]), (values_in.at[1], values.at[1]), (coords_in, coords),
    )):
        moves.append(pltpu.make_async_copy(source, target, sems.at[n]))
        moves[n].start()
    moves[0].wait()
    moves[1].wait()
    rows = three(items[...], 0)
    pairs = dot(rows, jnp.concatenate([table[:R]] * PACK), (0, 0))
    pairs *= dot(rows, jnp.concatenate([table[R:2 * R]] * PACK), (0, 0))
    table[TABLE.shape[0]:] = pairs.astype(bf16)
    irows[...] = four_a_row(dot(rows, fold(), (0, 0)))
    for slot in range(2):
        moves[2 + 2 * slot].wait()
        moves[3 + 2 * slot].wait()
        own = observed[slot].astype(f32)
        if slot > 0:
            own = jnp.where(counts[0, 0] > slot, own, 0.0)
        mask[slot] = own.astype(bf16).astype(jnp.float8_e4m3fn)
        weighted[slot] = (values[slot].astype(f32) * own).astype(bf16)
        turned[slot] = turn(own, strips).astype(turned.dtype)
    moves[6].wait()
    for slot in range(2):
        for n in range(3):
            places[slot, n] = coords[slot, n]


def user_kernel(places, weeks, mask, weighted, irows, table, out, wpairs, moment):
    one, two, put = table[:R], table[R:2 * R], table[2 * R:TABLE.shape[0]]
    pairs, rows = week_blocks(weeks, one, two, [places[slot, 2] for slot in range(2)])
    out[...] = jnp.zeros_like(out)
    apart = iota((CHUNK, LANES), 0) // B == iota((CHUNK, LANES), 1) // R
    gram, rhs = [], []
    for slot in range(2):
        ibase = pl.multiple_of(places[slot, 1] * B, B)
        wp, wr = pairs[slot * B:(slot + 1) * B], rows[slot * B:(slot + 1) * B]
        wpairs[slot] = wp
        ip = table[pl.ds(pl.multiple_of(TABLE.shape[0] + ibase, B), B), :].astype(f32)
        ir = irows[pl.ds(pl.multiple_of(places[slot, 1] * (B // PACK), B // PACK), B // PACK), :]
        every = jnp.concatenate([weighted[slot, :, c * CHUNK:(c + 1) * CHUNK] for c in range(B // SIDE)])
        every = dot(every, jnp.where(apart, jnp.concatenate([wr] * SIDE), 0.0).astype(bf16))
        total = jnp.zeros((B, LANES), f32)
        for c in range(B // SIDE):
            here = every[c * B:(c + 1) * B]
            moment[slot, c] = here
            total += here * ir[c:c + 1]
        rhs.append(total)
        gram.append(paired(mask, slot, ip, wp.reshape(B // 16, 16, WIDTH)))
    same = places[0, 0] == places[1, 0]
    rhs = unfold(jnp.concatenate(together(*rhs, same)))
    sent = send_form(jnp.concatenate(together(*gram, same)), rhs, put)
    for slot in range(2):
        out[pl.ds(pl.multiple_of(places[slot, 0] * B, B), B), :] = sent[slot * B:(slot + 1) * B]


def item_kernel(places, turned, moment, users, wpairs, table, out):
    one, two, put = table[:R], table[R:2 * R], table[2 * R:TABLE.shape[0]]
    rows = jnp.concatenate([users[pl.ds(pl.multiple_of(places[slot, 0] * B, B), B), :] for slot in range(2)])
    pairs = dot(rows, jnp.concatenate([one] * PACK)) * dot(rows, jnp.concatenate([two] * PACK))
    rows = dot(rows, fold())
    out[...] = jnp.zeros_like(out)
    gram, sums = [], []
    for slot in range(2):
        here = slice(slot * B, (slot + 1) * B)
        gram.append(paired(turned, slot, pairs[here], wpairs[slot].reshape(B // 16, 16, WIDTH)))
        sums.append(jnp.sum(moment[slot] * rows[here][None], axis=1))
    parts = three(jnp.concatenate(sums), 0)
    count = 2 * B
    spread = iota((count, count), 1) % (count // PACK) == iota((count, count), 0) // PACK
    rhs = dot(jnp.where(spread, 1.0, 0.0).astype(bf16), parts)
    rhs = jnp.where(iota(rhs.shape, 0) % PACK == iota(rhs.shape, 1) // R, rhs, 0.0)
    same = places[0, 1] == places[1, 1]
    rhs = jnp.concatenate(together(rhs[:B], rhs[B:], same))
    high = rhs.astype(bf16).astype(f32)
    parts = jnp.concatenate([high, rhs - high], axis=1).astype(bf16)
    wide = jnp.concatenate([put[:R]] * PACK + [put[R:]] * PACK)
    sent = (jnp.concatenate(together(*gram, same)) + dot(parts, wide)).astype(LINK)
    for slot in range(2):
        out[pl.ds(pl.multiple_of(places[slot, 1] * B, B), B), :] = sent[slot * B:(slot + 1) * B]


def solve_kernel(parts, out, copies):
    count = parts.shape[0]
    pick = (iota((count, LANES), 0) % T == iota((count, LANES), 1)).astype(f32)
    if LINK == bf16:
        packed = dot(parts[...], pick.astype(bf16), (0, 0))
    else:
        packed = dot(parts[...], pick, (0, 0), precise)
    sub = iota((T, LANES), 0)

    def tile(r, t):
        first = START[r] + (t - r // T) * T
        return packed[first:first + T]

    def spread(x, n):
        return jnp.broadcast_to(x[n:n + 1], (T, LANES))

    tiles = R // T
    rows = {}
    for r in range(R):
        for t in range(r // T, tiles):
            x = tile(r, t)
            rows[r, t] = x + jnp.where(sub == r % T, ridge_weight, 0.0) if t == r // T else x
    side = []
    for j in range(tiles):
        row5, row6, row7 = (tile(j * T + n, j) for n in (5, 6, 7))
        high = jnp.where(sub == 7, spread(row6, 0), row7)
        low = jnp.where(sub == 0, row5, row6)
        low = jnp.where(sub == 6, spread(row5, 1), low)
        low = jnp.where(sub == 7, spread(row5, 2), low)
        side.append(high + low)
    factor, right = {}, []
    for k in range(R):
        own = k // T
        inverse = 1.0 / spread(rows[k, own], k % T)
        mine = spread(side[own], k % T)
        right.append(mine * inverse)
        for t in range(own, tiles):
            side[t] = side[t] - rows[k, t] * right[k]
        for r in range(k + 1, R):
            factor[k, r] = spread(rows[k, r // T], r % T) * inverse
            for t in range(r // T, tiles):
                rows[r, t] = rows[r, t] - factor[k, r] * rows[k, t]
    answer = []
    for s in range(R - 1, -1, -1):
        for k in range(s):
            right[k] = right[k] - factor[k, s] * right[s]
    for j in range(tiles):
        x = right[j * T]
        for n in range(1, T):
            x = jnp.where(sub == n, right[j * T + n], x)
        answer.append(x)
    answer = jnp.concatenate(answer + [jnp.zeros((LANES - R, LANES), f32)], axis=0)
    answer = jnp.transpose(answer)[:T]
    out[...] = answer[:, :R]
    if copies.dtype == bf16:
        answer = three(answer[:, :R], 1).astype(f32)
        copies[...] = jnp.concatenate([answer] * (copies.shape[0] // T)).astype(bf16)
    else:
        copies[...] = jnp.broadcast_to(answer[None], copies.shape)


def vmem():
    return pl.BlockSpec(memory_space=pltpu.VMEM)


def smem():
    return pl.BlockSpec(memory_space=pltpu.SMEM)


def anywhere():
    return pl.BlockSpec(memory_space=pl.ANY)


def params(mib):
    return pltpu.CompilerParams(vmem_limit_bytes=mib * 1024 * 1024)


def prepare(coords, counts, values, observed, items, table):
    coords, values, observed, items, table = (
        pltpu.with_memory_space_constraint(x, pltpu.HBM) for x in (coords, values, observed, items, table)
    )
    return pl.pallas_call(
        prepare_kernel,
        out_shape=(
            pltpu.VMEM(values.shape, jnp.float8_e4m3fn),
            pltpu.VMEM(values.shape, jnp.float8_e4m3fn),
            pltpu.VMEM(values.shape, bf16),
            pltpu.VMEM((IBD * B // PACK, LANES), f32),
            pltpu.VMEM((table.shape[0] + IBD * B, WIDTH), bf16),
            jax.ShapeDtypeStruct((2, 3), jnp.int32),
        ),
        in_specs=[anywhere(), smem()] + [anywhere()] * 4,
        out_specs=[vmem()] * 5 + [smem()],
        scratch_shapes=[
            pltpu.SMEM(coords.shape, jnp.int32), pltpu.VMEM(values.shape, bf16), pltpu.VMEM(observed.shape, jnp.int32), pltpu.VMEM(items.shape, f32),
            pltpu.VMEM((B * B // 2 + B, LANES), f32), pltpu.SemaphoreType.DMA((7,)),
        ],
        compiler_params=params(16),
    )(coords, counts, values, observed, items, table)


def user_equations(places, weeks, mask, weighted, irows, table):
    return pl.pallas_call(
        user_kernel,
        out_shape=(
            pltpu.VMEM((UBD * B, WIDTH), LINK),
            pltpu.VMEM((2, B, WIDTH), bf16),
            pltpu.VMEM((2, B // SIDE, B, LANES), f32),
        ),
        in_specs=[smem()] + [vmem()] * 5,
        out_specs=[vmem()] * 3,
        compiler_params=params(16),
    )(places, weeks, mask, weighted, irows, table)


def item_equations(places, turned, moment, users, wpairs, table):
    return pl.pallas_call(
        item_kernel,
        out_shape=pltpu.VMEM((IBD * B, WIDTH), LINK),
        in_specs=[smem()] + [vmem()] * 5,
        out_specs=vmem(),
        compiler_params=params(16),
    )(places, turned, moment, users, wpairs, table)


def solve(parts, copies):
    return pl.pallas_call(
        solve_kernel,
        out_shape=(jax.ShapeDtypeStruct((T, R), f32), copies),
        in_specs=[vmem()],
        out_specs=(vmem(), vmem()),
        compiler_params=params(16),
    )(parts)


def week_kernel(weeks, out):
    rows = weeks[...]
    row = jnp.concatenate([
        jnp.concatenate([rows[k * PACK + n:k * PACK + n + 1] for n in range(PACK)], axis=1) for k in range(2)
    ], axis=0)
    out[...] = jnp.broadcast_to(row[None], out.shape).astype(bf16)


def week_copies(weeks, peers):
    return pl.pallas_call(
        week_kernel,
        out_shape=pltpu.VMEM((peers, 2, LANES), bf16),
        in_specs=[vmem()],
        out_specs=vmem(),
        compiler_params=params(16),
    )(weeks)


def copies_kernel(x, out):
    rows = x[...].reshape(out.shape[1:])
    out[...] = jnp.broadcast_to(rows[None], out.shape)


def copies_of(x, peers):
    return pl.pallas_call(
        copies_kernel,
        out_shape=pltpu.VMEM((peers, x.shape[0], LANES), x.dtype),
        in_specs=[vmem()],
        out_specs=vmem(),
        compiler_params=params(16),
    )(x)


def exchange(x, axis):
    return lax.all_to_all(x, axis, 0, 0, tiled=True)


def shards(values, observed, coords, counts, item_factors, week_factors):
    n_slab, n_fib = lax.axis_size(SLABS), lax.axis_size(FIBS)
    pair = lax.all_gather(week_factors, "core", axis=0, tiled=True)
    copies = week_copies(pair, n_slab * n_fib // 2)
    weeks = exchange(copies, ("z", "x", "y"))
    mask, turned, weighted, irows, table, places = prepare(
        coords[0], counts, values[0], observed[0], item_factors.T, jnp.asarray(TABLE, bf16)
    )
    parts, wpairs, moment = user_equations(places, weeks, mask, weighted, irows, table)
    user_out, copies = solve(exchange(parts, FIBS), pltpu.VMEM((n_fib * T, LANES), bf16))
    users = exchange(copies, FIBS)
    parts = item_equations(places, turned, moment, users, wpairs, table)
    _, copies = solve(exchange(parts, SLABS), pltpu.VMEM((n_slab, T, LANES), f32))
    item_updated = exchange(copies, SLABS).reshape(IBD * B, LANES)[:, :R]
    return (user_out, item_updated)


def solution(mesh):
    fine = jax.sharding.Mesh(mesh.devices.reshape(8, 2, 4, 8), SLABS + FIBS)
    in_specs = (
        P(SLABS, FIBS, None, None),
        P(SLABS, FIBS, None, None),
        P(SLABS, FIBS, None),
        P(SLABS, FIBS),
        P(FIBS, None),
        P(SLABS + FIBS, None),
    )
    out_specs = (P(SLABS + FIBS, None), P(FIBS, None))
    return jax.shard_map(shards, mesh=fine, in_specs=in_specs, out_specs=out_specs, check_vma=False)
```
